128 devices in a mesh: seq: 16 (over z, x), tp: 2 (over core), dp: 4 (over y).
Axes of the slice: x: 4, y: 4, z: 4, core: 2. Of those that a mesh axis runs over, the one named last changes fastest.
Arguments:
- media_tokens: bfloat16 [4, 8192, 1408], P('dp', 'seq'), as said below
- latents: bfloat16 [1024, 1408], replicated, as said below
- query_weight: bfloat16 [1408, 1408], P(None, 'tp'), as said below
- key_weight: bfloat16 [1408, 1408], P(None, 'tp'), as said below
- value_weight: bfloat16 [1408, 1408], P(None, 'tp'), may hold values from -0.15625 to 0.15625
- out_weight: bfloat16 [1408, 1408], P('tp'), may hold values from -0.15625 to 0.15625
- cotangent: bfloat16 [4, 1024, 1408], P('dp'), may hold values from -6 to 6
Outputs:
- resampled: bfloat16 [4, 1024, 1408], P('dp', None, 'tp')
- grad_latents: float32 [1024, 1408], P('seq', ('tp', 'dp'))
- grad_query: float32 [1408, 1408], P(('seq', 'dp'), 'tp')
- grad_key: float32 [1408, 1408], P(('seq', 'dp'), 'tp')
- grad_value: float32 [1408, 1408], P(('seq', 'dp'), 'tp')
- grad_out: float32 [1408, 1408], P('tp', ('seq', 'dp'))
The draws below stay inside these ranges and needn't reach their ends.
Inputs may be any that keep to these rules, and one draw needn't show every extreme that they name: `media_tokens`: video features of order one. `latents`: latent entries of order one. `query_weight`: entries of order 1408^-0.5. `key_weight`: entries of order 1408^-0.5.
All inputs are finite; a program needn't handle non-finite values.
Results may differ from the reference program's by a relative error of at most 0.034.
The reference program's roundings to bfloat16 on the way count: a program that leaves them out, or rounds other values in their place, can miss the bound.
Values sent between devices are 32-bit elements; how exact they have to be, the bound alone decides.
No kernel may reach another device: no remote copies, remote signals or barrier semaphores. Data moves between devices by JAX's collectives and lax.ppermute only.
A program may use at most 192 MiB of HBM per device.

```python
import math
import jax
import jax.numpy as jnp
from jax import lax

D = 1408
H = 16
HD = 88
L = 1024
TOKENS = 8192
VIDEOS = 4


def latent_base(key):
    return jnp.clip(jax.random.normal(key, (L, D), jnp.float32), -5.0, 5.0)


def shared_matrix(key):
    return jnp.clip(jax.random.normal(key, (D, D), jnp.float32), -5.0, 5.0)


def draw_latents(key, part):
    base = latent_base(key)
    rows = base
    return rows.astype(jnp.bfloat16)


def draw_media_tokens(key, part):
    key = jax.random.fold_in(key, 2)
    filled = jnp.clip(jax.random.normal(key, (VIDEOS, TOKENS, D), jnp.float32), -6.0, 6.0)
    return filled.astype(jnp.bfloat16)


def draw_query_weight(key, part):
    shared = shared_matrix(key)
    key = jax.random.fold_in(key, 3)
    own = jnp.clip(jax.random.normal(key, (D, D), jnp.float32), -5.0, 5.0)
    mixed = 1.5 * (0.6 * shared + 0.8 * own)
    return (mixed / math.sqrt(D)).astype(jnp.bfloat16)


def draw_key_weight(key, part):
    shared = shared_matrix(key)
    key = jax.random.fold_in(key, 4)
    own = jnp.clip(jax.random.normal(key, (D, D), jnp.float32), -5.0, 5.0)
    mixed = 0.6 * shared + 0.8 * own
    return (mixed / math.sqrt(D)).astype(jnp.bfloat16)


def levels(own_key, dims, shards, low, high):
    level = 1.0
    for position, parts in shards:
        steps = jax.random.uniform(jax.random.fold_in(jax.random.fold_in(own_key, 6), position), (parts,), jnp.float32, low / len(shards), high / len(shards))
        level = level * jnp.repeat(jnp.exp(steps), dims[position] // parts).reshape((-1,) + (1,) * (len(dims) - 1 - position))
    return level


def centred(key, shape, width, limit, shards=(), dtype=jnp.bfloat16):
    array = width * jax.random.normal(key, shape, jnp.float32)
    if shards:
        array = array * levels(key, shape, shards, -0.22, 0.18)
    return jnp.clip(array, -limit, limit).astype(dtype)


def setup_inputs(seed: int = 0) -> dict:
    seeds = jax.random.split(jax.random.key(seed), 8)
    media_tokens = draw_media_tokens(jax.random.fold_in(seeds[7], 71), 0)
    latents = draw_latents(jax.random.fold_in(seeds[7], 71), 0)
    query_weight = draw_query_weight(jax.random.fold_in(seeds[7], 71), 0)
    key_weight = draw_key_weight(jax.random.fold_in(seeds[7], 71), 0)
    value_weight = centred(seeds[4], (D, D), D ** -0.5, 0.15625, ((1, 2),))
    out_weight = centred(seeds[5], (D, D), D ** -0.5, 0.15625, ((0, 2),))
    cotangent = centred(seeds[6], (VIDEOS, L, D), 1.0, 6.0, ((0, 4),))
    return {"media_tokens": media_tokens, "latents": latents, "query_weight": query_weight, "key_weight": key_weight, "value_weight": value_weight, "out_weight": out_weight, "cotangent": cotangent}


def layer_norm(rows):
    average = lax.optimization_barrier(jnp.mean(rows, -1, keepdims=True))
    centered = rows - average
    variance = lax.optimization_barrier(jnp.mean(centered * centered, -1, keepdims=True))
    inv_std = lax.rsqrt(variance + 1e-05)
    return (centered * inv_std, inv_std)

def norm_backward(normed, inv_std, upstream):
    mean_up = lax.optimization_barrier(jnp.mean(upstream, -1, keepdims=True))
    mean_cross = lax.optimization_barrier(jnp.mean(upstream * normed, -1, keepdims=True))
    return inv_std * (upstream - mean_up - normed * mean_cross)

def reference(media_tokens, latents, query_weight, key_weight, value_weight, out_weight, cotangent):
    head_scale = HD ** (-0.5)
    latent_f = latents.astype(jnp.float32)
    latent_hat, latent_inv = layer_norm(latent_f)
    latent_norm = latent_hat.astype(jnp.bfloat16)
    queries = (jnp.dot(latent_norm, query_weight, preferred_element_type=jnp.float32) * head_scale).astype(jnp.bfloat16)

    def split_heads(matrix):
        return matrix.reshape(matrix.shape[0], H, HD).transpose(1, 0, 2)

    def join_heads(stacked):
        return stacked.transpose(1, 0, 2).reshape(stacked.shape[1], D)
    query_heads = split_heads(queries)

    def per_head(operands):
        query_head, key_head, value_head, upstream_head = operands
        scores = jnp.dot(query_head, key_head.T, preferred_element_type=jnp.float32)
        row_max = lax.optimization_barrier(jnp.max(scores, -1, keepdims=True))
        weights = jnp.exp(scores - row_max)
        row_sum = lax.optimization_barrier(jnp.sum(weights, -1, keepdims=True))
        weighted = jnp.dot(weights.astype(jnp.bfloat16), value_head, preferred_element_type=jnp.float32)
        attended = (weighted / row_sum).astype(jnp.bfloat16)
        row_delta = lax.optimization_barrier(jnp.sum(upstream_head.astype(jnp.float32) * attended.astype(jnp.float32), -1, keepdims=True))
        probs = weights / row_sum
        prob_grad = jnp.dot(upstream_head, value_head.T, preferred_element_type=jnp.float32)
        score_grad = (probs * (prob_grad - row_delta)).astype(jnp.bfloat16)
        value_grad = jnp.dot(probs.astype(jnp.bfloat16).T, upstream_head, preferred_element_type=jnp.float32).astype(jnp.bfloat16)
        key_grad = jnp.dot(score_grad.T, query_head, preferred_element_type=jnp.float32).astype(jnp.bfloat16)
        query_grad = jnp.dot(score_grad, key_head, preferred_element_type=jnp.float32)
        return (attended, value_grad, key_grad, query_grad)

    def per_video(operands):
        media_rows, upstream_rows = operands
        normed, unused_inv = layer_norm(media_rows.astype(jnp.float32))
        media_norm = normed.astype(jnp.bfloat16)
        key_rows = jnp.dot(media_norm, key_weight, preferred_element_type=jnp.float32).astype(jnp.bfloat16)
        value_rows = jnp.dot(media_norm, value_weight, preferred_element_type=jnp.float32).astype(jnp.bfloat16)
        upstream_att = jnp.dot(upstream_rows, out_weight.T, preferred_element_type=jnp.float32).astype(jnp.bfloat16)
        attended, value_grad, key_grad, query_grad = lax.map(per_head, (query_heads, split_heads(key_rows), split_heads(value_rows), split_heads(upstream_att)))
        attended = join_heads(attended)
        resampled = (latent_f + jnp.dot(attended, out_weight, preferred_element_type=jnp.float32)).astype(jnp.bfloat16)
        grad_key = jnp.dot(media_norm.T, join_heads(key_grad), preferred_element_type=jnp.float32)
        grad_value = jnp.dot(media_norm.T, join_heads(value_grad), preferred_element_type=jnp.float32)
        query_proj = (join_heads(query_grad) * head_scale).astype(jnp.bfloat16)
        grad_query = jnp.dot(latent_norm.T, query_proj, preferred_element_type=jnp.float32)
        grad_out = jnp.dot(attended.T, upstream_rows, preferred_element_type=jnp.float32)
        latent_up = jnp.dot(query_proj, query_weight.T, preferred_element_type=jnp.float32)
        grad_latent = upstream_rows.astype(jnp.float32) + norm_backward(latent_hat, latent_inv, latent_up)
        return (resampled, grad_latent, grad_query, grad_key, grad_value, grad_out)
    results = lax.map(per_video, (media_tokens, cotangent))
    return (results[0], lax.optimization_barrier(jnp.sum(results[1], 0)), lax.optimization_barrier(jnp.sum(results[2], 0)), lax.optimization_barrier(jnp.sum(results[3], 0)), lax.optimization_barrier(jnp.sum(results[4], 0)), lax.optimization_barrier(jnp.sum(results[5], 0)))
```

```python
import functools

import jax
import jax.numpy as jnp
from jax import lax
from jax.experimental import pallas as pl
from jax.experimental.pallas import tpu as pltpu
from jax.sharding import PartitionSpec as P

HD = 88
VMEM = 56 * 1024 * 1024
F32 = jnp.float32
BF16 = jnp.bfloat16
NT = (((1,), (1,)), ((), ()))
TN = (((0,), (0,)), ((), ()))


def params():
    return pltpu.CompilerParams(vmem_limit_bytes=VMEM)


def cost(flops, size):
    return pl.CostEstimate(flops=int(flops), bytes_accessed=int(size), transcendentals=0)


def dot(a, b, dims=(((1,), (0,)), ((), ()))):
    return lax.dot_general(a, b, dims, preferred_element_type=F32)


def layer_norm(rows):
    average = jnp.mean(rows, -1, keepdims=True)
    centered = rows - average
    variance = jnp.mean(centered * centered, -1, keepdims=True)
    inv_std = lax.rsqrt(variance + 1e-05)
    return (centered * inv_std, inv_std)


def norm_backward(normed, inv_std, upstream):
    mean_up = jnp.mean(upstream, -1, keepdims=True)
    mean_cross = jnp.mean(upstream * normed, -1, keepdims=True)
    return inv_std * (upstream - mean_up - normed * mean_cross)


def project_kernel(
    media_ref, latents_ref, cot_ref, qw_ref, kw_ref, vw_ref, ow_ref,
    mn_ref, ln_ref, q_ref, k_ref, v_ref, u_ref,
):
    def split(ref, value):
        for head in range(ref.shape[0]):
            ref[head] = value[head * HD : (head + 1) * HD, :].astype(BF16)

    media_norm = layer_norm(media_ref[...].astype(F32))[0].T.astype(BF16)
    mn_ref[...] = media_norm
    split(k_ref, dot(kw_ref[...], media_norm))
    split(v_ref, dot(vw_ref[...], media_norm))
    latent_norm = layer_norm(latents_ref[...].astype(F32))[0].T.astype(BF16)
    ln_ref[...] = latent_norm
    split(q_ref, dot(qw_ref[...], latent_norm) * HD ** (-0.5))
    split(u_ref, dot(ow_ref[...], cot_ref[...], NT))


def project(media, latents, cot, qw, kw, vw, ow):
    tokens, width = media.shape
    count = latents.shape[0]
    inner = qw.shape[0]
    heads = inner // HD
    steps = 2
    t, c = tokens // steps, count // steps
    rows = lambda n: pl.BlockSpec((n, width), lambda i: (i, 0))
    cols = lambda n: pl.BlockSpec((width, n), lambda i: (0, i))
    whole = lambda a: pl.BlockSpec(a.shape, lambda i: (0, 0))
    turned = lambda n: pl.BlockSpec((heads, HD, n), lambda i: (0, 0, i))
    shape = jax.ShapeDtypeStruct
    return pl.pallas_call(
        project_kernel,
        grid=(steps,),
        in_specs=[rows(t), rows(c), rows(c), whole(qw), whole(kw), whole(vw), whole(ow)],
        out_specs=[cols(t), cols(c), turned(c), turned(t), turned(t), turned(c)],
        out_shape=[
            shape((width, tokens), BF16),
            shape((width, count), BF16),
            shape((heads, HD, count), BF16),
            shape((heads, HD, tokens), BF16),
            shape((heads, HD, tokens), BF16),
            shape((heads, HD, count), BF16),
        ],
        compiler_params=params(),
        cost_estimate=cost(4 * (tokens + count) * width * inner, 24e6),
        name="project",
    )(media, latents, cot, qw, kw, vw, ow)


def forward_kernel(chunk, q_ref, k_ref, v_ref, u_ref, w_ref, stat_ref):
    head = pl.program_id(0)
    count = q_ref.shape[2]
    half = count // 2
    keys = k_ref[0].astype(F32).T.astype(BF16)
    vals = v_ref[0]
    for start in range(0, count, chunk):
        cols = slice(start, start + chunk)
        scores = dot(keys, q_ref[0, :, cols])
        top = jnp.max(scores, 0, keepdims=True)
        weights = jnp.exp(scores - top)
        total = jnp.sum(weights, 0, keepdims=True)
        weighted = dot(vals, weights.astype(BF16))
        delta = jnp.sum(u_ref[0, :, cols].astype(F32) * weighted, 0, keepdims=True)
        side, inner = divmod(start, half)
        w_ref[side, 0, :, inner : inner + chunk] = weighted
        stat_ref[0, pl.ds(head, 1), cols] = top
        stat_ref[1, pl.ds(head, 1), cols] = total
        stat_ref[2, pl.ds(head, 1), cols] = delta


def forward(q, k, v, u):
    heads, _, count = q.shape
    tokens = k.shape[2]
    per_head = lambda n: pl.BlockSpec((1, HD, n), lambda h: (h, 0, 0))
    return pl.pallas_call(
        functools.partial(forward_kernel, min(256, count // 2)),
        grid=(heads,),
        in_specs=[per_head(count), per_head(tokens), per_head(tokens), per_head(count)],
        out_specs=[
            pl.BlockSpec((2, 1, HD, count // 2), lambda h: (0, h, 0, 0)),
            pl.BlockSpec((3, heads, count), lambda h: (0, 0, 0)),
        ],
        out_shape=[
            jax.ShapeDtypeStruct((2, heads, HD, count // 2), F32),
            jax.ShapeDtypeStruct((3, heads, count), F32),
        ],
        compiler_params=params(),
        cost_estimate=cost(16 * heads * count * tokens * HD, 9e6),
        name="attend",
    )(q, k, v, u)


def backward_kernel(
    chunk, q_ref, k_ref, v_ref, u_ref, lse_ref, delta_ref, dq_ref, dk_ref, dv_ref, done_ref
):
    head = pl.program_id(0)
    count = q_ref.shape[2]
    half = count // 2
    keys_t = k_ref[0]
    keys = keys_t.astype(F32).T.astype(BF16)
    vals = v_ref[0].astype(F32).T.astype(BF16)
    key_grad = jnp.zeros(keys.shape, F32)
    value_grad = jnp.zeros(vals.shape, F32)
    for start in range(0, count, chunk):
        cols = slice(start, start + chunk)
        q = q_ref[0, :, cols]
        u = u_ref[0, :, cols]
        probs = jnp.exp(dot(keys, q) - lse_ref[pl.ds(head, 1), cols])
        grad = (probs * (dot(vals, u) - delta_ref[pl.ds(head, 1), cols])).astype(BF16)
        value_grad += dot(probs.astype(BF16), u.astype(F32).T.astype(BF16))
        key_grad += dot(grad, q.astype(F32).T.astype(BF16))
        side, inner = divmod(start, half)
        dq_ref[side, 0, :, inner : inner + chunk] = dot(keys_t, grad)
    dk_ref[0] = key_grad.T.astype(BF16)
    dv_ref[0] = value_grad.T.astype(BF16)
    done_ref[...] = jnp.zeros_like(done_ref)


def backward(q, k, v, u, lse, delta):
    heads, _, count = q.shape
    tokens = k.shape[2]
    per_head = lambda n: pl.BlockSpec((1, HD, n), lambda h: (h, 0, 0))
    whole = pl.BlockSpec((heads, count), lambda h: (0, 0))
    return pl.pallas_call(
        functools.partial(backward_kernel, min(256, count // 2)),
        grid=(heads,),
        in_specs=[
            per_head(count), per_head(tokens), per_head(tokens), per_head(count), whole, whole,
        ],
        out_specs=[
            pl.BlockSpec((2, 1, HD, count // 2), lambda h: (0, h, 0, 0)),
            per_head(tokens),
            per_head(tokens),
            pl.BlockSpec((8, 128), lambda h: (0, 0)),
        ],
        out_shape=[
            jax.ShapeDtypeStruct((2, heads, HD, count // 2), F32),
            jax.ShapeDtypeStruct((heads, HD, tokens), BF16),
            jax.ShapeDtypeStruct((heads, HD, tokens), BF16),
            jax.ShapeDtypeStruct((8, 128), F32),
        ],
        compiler_params=params(),
        cost_estimate=cost(40 * heads * count * tokens * HD, 9e6),
        name="attend_back",
    )(q, k, v, u, lse, delta)


def sum_kernel(pieces_ref, after_ref, out_ref):
    out_ref[...] = jnp.sum(pieces_ref[...], 0)


def sum_pieces(pieces, after):
    return pl.pallas_call(
        sum_kernel,
        out_shape=jax.ShapeDtypeStruct(pieces.shape[1:], F32),
        compiler_params=params(),
        cost_estimate=cost(pieces.size, 4 * pieces.size),
        name="sum_pieces",
    )(pieces, after)


def out_kernel(att_ref, rows_ref, own_ref, other_ref, grad_ref, keep_ref, send_ref):
    att = att_ref[0].reshape(own_ref.shape[1], att_ref.shape[3]).astype(BF16)
    term = dot(rows_ref[...], att, NT)

    @pl.when(pl.program_id(0) == 0)
    def _():
        grad_ref[...] = term

    @pl.when(pl.program_id(0) > 0)
    def _():
        grad_ref[...] += term

    send_ref[...] = dot(other_ref[...], att)
    keep_ref[...] = dot(own_ref[...], att)


def out_step(att, rows, own, other):
    _, heads, _, half = att.shape
    width, inner = own.shape
    share = rows.shape[0]
    whole = lambda a: pl.BlockSpec(a.shape, lambda i: (0, 0))
    return pl.pallas_call(
        out_kernel,
        grid=(2,),
        in_specs=[
            pl.BlockSpec((1, heads, HD, half), lambda i: (i, 0, 0, 0)),
            pl.BlockSpec((share, half), lambda i: (0, i)),
            whole(own),
            whole(other),
        ],
        out_specs=[
            pl.BlockSpec((share, inner), lambda i: (0, 0)),
            pl.BlockSpec((width, half), lambda i: (0, i)),
            pl.BlockSpec((width, half), lambda i: (0, i)),
        ],
        out_shape=[
            jax.ShapeDtypeStruct((share, inner), F32),
            jax.ShapeDtypeStruct((width, 2 * half), F32),
            jax.ShapeDtypeStruct((width, 2 * half), F32),
        ],
        compiler_params=params(),
        cost_estimate=cost(8 * half * inner * width, 12e6),
        name="project_out",
    )(att, rows, own, other)


def query_kernel(pieces_ref, norm_ref, total_ref, grad_ref):
    total = jnp.sum(pieces_ref[...], 0)
    total_ref[...] = total
    proj = (total * HD ** (-0.5)).astype(BF16)
    grad_ref[...] = dot(norm_ref[...], proj, NT)


def query_step(pieces, norm):
    _, depth, half = pieces.shape
    width = norm.shape[0]
    return pl.pallas_call(
        query_kernel,
        out_shape=[
            jax.ShapeDtypeStruct((depth, half), F32),
            jax.ShapeDtypeStruct((width, depth), F32),
        ],
        compiler_params=params(),
        cost_estimate=cost(2 * half * width * depth, 6e6),
        name="query_grad",
    )(pieces, norm)


def latent_kernel(pieces_ref, qw_ref, latents_ref, cot_ref, out_ref):
    heads, depth, rows = pieces_ref.shape
    proj = pieces_ref[...].reshape(heads * depth, rows) * HD ** (-0.5)
    up = dot(proj.T.astype(BF16), qw_ref[...])
    hat, inv = layer_norm(latents_ref[...].astype(F32))
    term = norm_backward(hat, inv, up) + cot_ref[...].astype(F32) / 2
    size = out_ref.shape[2]
    for block in range(out_ref.shape[0]):
        out_ref[block] = term[:, block * size : (block + 1) * size]


def latent_step(pieces, qw, latents, cot, blocks):
    rows, width = latents.shape
    return pl.pallas_call(
        latent_kernel,
        out_shape=jax.ShapeDtypeStruct((blocks, rows, width // blocks), F32),
        compiler_params=params(),
        cost_estimate=cost(2 * rows * qw.size, 4e6),
        name="latent_grad",
    )(pieces, qw, latents, cot)


def shift(value, axis, by, side=None, minor=True):
    size = lax.axis_size(axis)
    if side is None:
        pairs = [(i, (i + by) % size) for i in range(size)]
    elif minor:
        pairs = [(i, i // side * side + (i % side + by) % side) for i in range(size)]
    else:
        pairs = [(i, (i + by * side) % size) for i in range(size)]
    return lax.ppermute(value, axis, pairs)


def pick(blocks, index):
    return lax.dynamic_index_in_dim(blocks, index, 0, False)


def scatter_sum(blocks, axis, place):
    size = blocks.shape[0]
    total = pick(blocks, place)
    for by in range(1, size):
        total = total + shift(pick(blocks, (place + by) % size), axis, by)
    return total


def relay_sum(blocks, place, cut, send):
    far = pick(blocks, (place + 2) % 4)
    front = send(far[:cut], 1)
    back = send(far[cut:], -1)
    ahead = pick(blocks, (place + 1) % 4)
    behind = pick(blocks, (place + 3) % 4)
    ahead = jnp.concatenate([ahead[:cut] + front, ahead[cut:]], 0)
    behind = jnp.concatenate([behind[:cut], behind[cut:] + back], 0)
    return pick(blocks, place) + send(ahead, 1) + send(behind, -1)


def merge_stats(stats, side, minor):
    parts = [stats] + [shift(stats, "seq", by, side, minor) for by in range(1, side)]
    top = functools.reduce(jnp.maximum, [p[0] for p in parts])
    factors = [jnp.exp(p[0] - top) for p in parts]
    total = sum(p[1] * f for p, f in zip(parts, factors))
    delta = sum(p[2] * f for p, f in zip(parts, factors))
    return jnp.stack([top, total, delta])


def local(media_tokens, latents, query_weight, key_weight, value_weight, out_weight, cotangent):
    inner = query_weight.shape[1]
    width = query_weight.shape[0]
    heads = inner // HD
    count = latents.shape[0]
    half = count // 2
    seq, tp, dp = (lax.axis_index(a) for a in ("seq", "tp", "dp"))
    seqs, tps, dps = (lax.axis_size(a) for a in ("seq", "tp", "dp"))
    side = 4
    share = width // seqs
    part = share // dps
    padded = -(-part // 8) * 8
    rows = count // seqs
    upstream = cotangent[0]
    query_turned = query_weight.T

    media_norm, latent_norm, q, k, v, u = project(
        media_tokens[0], latents, upstream, query_turned, key_weight.T, value_weight.T, out_weight
    )
    weighted, stats = forward(q, k, v, u)

    near = merge_stats(stats, side, True)
    near, media_norm, latent_norm, cot, base, mix = lax.optimization_barrier(
        (near, media_norm, latent_norm, upstream, latents, out_weight)
    )
    blocks = media_norm.reshape(seqs, dps, part, -1).transpose(1, 0, 2, 3)
    blocks = jnp.pad(blocks, ((0, 0), (0, 0), (0, padded - part), (0, 0)))
    ready = (
        blocks.reshape(dps * seqs * padded, -1),
        lax.dynamic_slice_in_dim(latent_norm, seq // heads * half, half, 1),
        lax.dynamic_slice_in_dim(cot, seq * share, share, 1).T,
        lax.dynamic_slice_in_dim(mix, tp * inner, inner, 1).T,
        lax.dynamic_slice_in_dim(mix, (1 - tp) * inner, inner, 1).T,
        lax.dynamic_slice_in_dim(base, tp * inner, inner, 1).T,
        lax.dynamic_slice_in_dim(base, seq * rows, rows, 0),
        lax.dynamic_slice_in_dim(cot, seq * rows, rows, 0),
    )
    whole, ready = lax.optimization_barrier((merge_stats(near, side, False), ready))
    media_rows, norm_half, cot_cols, own, other, latent_cols, latent_rows, cot_rows = ready
    top, total, delta = whole
    lse = top + jnp.log(total)
    delta = delta / total
    factor = (jnp.exp(stats[0] - top) / total).reshape(heads, 2, 1, half).transpose(1, 0, 2, 3)

    scaled = (weighted * factor).reshape(seqs, HD, half)
    attended_pieces = lax.all_to_all(scaled, "seq", 0, 0, tiled=True)
    dq, dk, dv, done = backward(q, k, v, u, lse, delta)

    query_pieces = lax.all_to_all(dq.reshape(seqs, HD, half), "seq", 0, 0, tiled=True)

    ring = lambda value, by: shift(value, "dp", by)

    def weight_grad(grads):
        term = dot(media_rows, grads.reshape(inner, -1), NT)
        term = relay_sum(term.reshape(dps, seqs * padded, inner), dp, seqs * padded // 2, ring)
        return term.reshape(seqs, padded, inner)

    key_rows, value_rows = weight_grad(dk), weight_grad(dv)
    grad_key = jnp.sum(lax.all_to_all(key_rows, "seq", 0, 0, tiled=True), 0)[:part]
    grad_value = jnp.sum(lax.all_to_all(value_rows, "seq", 0, 0, tiled=True), 0)[:part]

    attended = lax.all_gather(sum_pieces(attended_pieces, done), "seq")
    out_rows, keep, away = out_step(attended.reshape(2, heads, HD, half), cot_cols, own, other)
    arrived = lax.ppermute(away, "tp", [(0, 1), (1, 0)])
    resampled = (latent_cols.astype(F32) + (keep + arrived)).astype(BF16).T[None]
    grad_out = scatter_sum(out_rows.reshape(dps, part, inner), "dp", dp).T

    query_total, term = query_step(query_pieces, norm_half)
    strips = query_total.reshape(HD, heads, rows).transpose(1, 0, 2)
    groups = [list(range(i * heads, (i + 1) * heads)) for i in range(2)]
    strips = lax.all_to_all(strips, "seq", 0, 0, axis_index_groups=groups, tiled=True)
    blocks = lax.all_to_all(term.reshape(seqs, share, HD), "seq", 0, 0, tiled=True)
    blocks = jnp.sum(blocks.reshape(2, heads, share, HD), 0).transpose(1, 0, 2)
    grad_query = scatter_sum(blocks.reshape(dps, part, inner), "dp", dp)
    term = latent_step(strips, query_turned, latent_rows, cot_rows, tps * dps)
    grad_latents = jnp.sum(lax.all_to_all(term, ("tp", "dp"), 0, 0, tiled=True), 0)
    return (resampled, grad_latents, grad_query, grad_key, grad_value, grad_out)


def solution(mesh):
    placed = (
        P("dp", "seq", None),
        P(),
        P(None, "tp"),
        P(None, "tp"),
        P(None, "tp"),
        P("tp", None),
        P("dp", None, None),
    )
    return jax.shard_map(
        local,
        mesh=mesh,
        in_specs=placed,
        out_specs=(
            P("dp", None, "tp"),
            P("seq", ("tp", "dp")),
            P(("seq", "dp"), "tp"),
            P(("seq", "dp"), "tp"),
            P(("seq", "dp"), "tp"),
            P("tp", ("seq", "dp")),
        ),
        check_vma=False,
    )
```

```python
import functools

import jax
import jax.numpy as jnp
from jax import lax
from jax.experimental import pallas as pl
from jax.experimental.pallas import tpu as pltpu
from jax.sharding import PartitionSpec as P

HD = 88
VMEM = 56 * 1024 * 1024
F32 = jnp.float32
BF16 = jnp.bfloat16
NT = (((1,), (1,)), ((), ()))
TN = (((0,), (0,)), ((), ()))


def params():
    return pltpu.CompilerParams(vmem_limit_bytes=VMEM)


def cost(flops, size):
    return pl.CostEstimate(flops=int(flops), bytes_accessed=int(size), transcendentals=0)


def dot(a, b, dims=(((1,), (0,)), ((), ()))):
    return lax.dot_general(a, b, dims, preferred_element_type=F32)


def layer_norm(rows):
    average = jnp.mean(rows, -1, keepdims=True)
    centered = rows - average
    variance = jnp.mean(centered * centered, -1, keepdims=True)
    inv_std = lax.rsqrt(variance + 1e-05)
    return (centered * inv_std, inv_std)


def norm_backward(normed, inv_std, upstream):
    mean_up = jnp.mean(upstream, -1, keepdims=True)
    mean_cross = jnp.mean(upstream * normed, -1, keepdims=True)
    return inv_std * (upstream - mean_up - normed * mean_cross)


def project_kernel(
    media_ref, latents_ref, cot_ref, qw_ref, kw_ref, vw_ref, ow_ref,
    mn_ref, ln_ref, q_ref, k_ref, v_ref, u_ref,
):
    def split(ref, value):
        for head in range(ref.shape[0]):
            ref[head] = value[head * HD : (head + 1) * HD, :].astype(BF16)

    media_norm = layer_norm(media_ref[...].astype(F32))[0].T.astype(BF16)
    mn_ref[...] = media_norm
    split(k_ref, dot(kw_ref[...], media_norm))
    split(v_ref, dot(vw_ref[...], media_norm))
    latent_norm = layer_norm(latents_ref[...].astype(F32))[0].T.astype(BF16)
    ln_ref[...] = latent_norm
    split(q_ref, dot(qw_ref[...], latent_norm) * HD ** (-0.5))
    split(u_ref, dot(ow_ref[...], cot_ref[...], NT))


def project(media, latents, cot, qw, kw, vw, ow):
    tokens, width = media.shape
    count = latents.shape[0]
    inner = qw.shape[0]
    heads = inner // HD
    steps = 2
    t, c = tokens // steps, count // steps
    rows = lambda n: pl.BlockSpec((n, width), lambda i: (i, 0))
    cols = lambda n: pl.BlockSpec((width, n), lambda i: (0, i))
    whole = lambda a: pl.BlockSpec(a.shape, lambda i: (0, 0))
    turned = lambda n: pl.BlockSpec((heads, HD, n), lambda i: (0, 0, i))
    shape = jax.ShapeDtypeStruct
    return pl.pallas_call(
        project_kernel,
        grid=(steps,),
        in_specs=[rows(t), rows(c), rows(c), whole(qw), whole(kw), whole(vw), whole(ow)],
        out_specs=[cols(t), cols(c), turned(c), turned(t), turned(t), turned(c)],
        out_shape=[
            shape((width, tokens), BF16),
            shape((width, count), BF16),
            shape((heads, HD, count), BF16),
            shape((heads, HD, tokens), BF16),
            shape((heads, HD, tokens), BF16),
            shape((heads, HD, count), BF16),
        ],
        compiler_params=params(),
        cost_estimate=cost(4 * (tokens + count) * width * inner, 24e6),
        name="project",
    )(media, latents, cot, qw, kw, vw, ow)


def forward_kernel(chunk, q_ref, k_ref, v_ref, u_ref, w_ref, stat_ref):
    head = pl.program_id(0)
    count = q_ref.shape[2]
    half = count // 2
    keys = k_ref[0].astype(F32).T.astype(BF16)
    vals = v_ref[0]
    for start in range(0, count, chunk):
        cols = slice(start, start + chunk)
        scores = dot(keys, q_ref[0, :, cols])
        top = jnp.max(scores, 0, keepdims=True)
        weights = jnp.exp(scores - top)
        total = jnp.sum(weights, 0, keepdims=True)
        weighted = dot(vals, weights.astype(BF16))
        delta = jnp.sum(u_ref[0, :, cols].astype(F32) * weighted, 0, keepdims=True)
        side, inner = divmod(start, half)
        w_ref[side, 0, :, inner : inner + chunk] = weighted
        stat_ref[0, pl.ds(head, 1), cols] = top
        stat_ref[1, pl.ds(head, 1), cols] = total
        stat_ref[2, pl.ds(head, 1), cols] = delta


def forward(q, k, v, u):
    heads, _, count = q.shape
    tokens = k.shape[2]
    per_head = lambda n: pl.BlockSpec((1, HD, n), lambda h: (h, 0, 0))
    return pl.pallas_call(
        functools.partial(forward_kernel, min(256, count // 2)),
        grid=(heads,),
        in_specs=[per_head(count), per_head(tokens), per_head(tokens), per_head(count)],
        out_specs=[
            pl.BlockSpec((2, 1, HD, count // 2), lambda h: (0, h, 0, 0)),
            pl.BlockSpec((3, heads, count), lambda h: (0, 0, 0)),
        ],
        out_shape=[
            jax.ShapeDtypeStruct((2, heads, HD, count // 2), F32),
            jax.ShapeDtypeStruct((3, heads, count), F32),
        ],
        compiler_params=params(),
        cost_estimate=cost(16 * heads * count * tokens * HD, 9e6),
        name="attend",
    )(q, k, v, u)


def backward_kernel(
    chunk, q_ref, k_ref, v_ref, u_ref, lse_ref, delta_ref, dq_ref, dk_ref, dv_ref, done_ref
):
    head = pl.program_id(0)
    count = q_ref.shape[2]
    half = count // 2
    keys_t = k_ref[0]
    keys = keys_t.astype(F32).T.astype(BF16)
    vals = v_ref[0].astype(F32).T.astype(BF16)
    key_grad = jnp.zeros(keys.shape, F32)
    value_grad = jnp.zeros(vals.shape, F32)
    for start in range(0, count, chunk):
        cols = slice(start, start + chunk)
        q = q_ref[0, :, cols]
        u = u_ref[0, :, cols]
        probs = jnp.exp(dot(keys, q) - lse_ref[pl.ds(head, 1), cols])
        grad = (probs * (dot(vals, u) - delta_ref[pl.ds(head, 1), cols])).astype(BF16)
        value_grad += dot(probs.astype(BF16), u.astype(F32).T.astype(BF16))
        key_grad += dot(grad, q.astype(F32).T.astype(BF16))
        side, inner = divmod(start, half)
        dq_ref[side, 0, :, inner : inner + chunk] = dot(keys_t, grad)
    dk_ref[0] = key_grad.T.astype(BF16)
    dv_ref[0] = value_grad.T.astype(BF16)
    done_ref[...] = jnp.zeros_like(done_ref)


def backward(q, k, v, u, lse, delta):
    heads, _, count = q.shape
    tokens = k.shape[2]
    per_head = lambda n: pl.BlockSpec((1, HD, n), lambda h: (h, 0, 0))
    whole = pl.BlockSpec((heads, count), lambda h: (0, 0))
    return pl.pallas_call(
        functools.partial(backward_kernel, min(256, count // 2)),
        grid=(heads,),
        in_specs=[
            per_head(count), per_head(tokens), per_head(tokens), per_head(count), whole, whole,
        ],
        out_specs=[
            pl.BlockSpec((2, 1, HD, count // 2), lambda h: (0, h, 0, 0)),
            per_head(tokens),
            per_head(tokens),
            pl.BlockSpec((8, 128), lambda h: (0, 0)),
        ],
        out_shape=[
            jax.ShapeDtypeStruct((2, heads, HD, count // 2), F32),
            jax.ShapeDtypeStruct((heads, HD, tokens), BF16),
            jax.ShapeDtypeStruct((heads, HD, tokens), BF16),
            jax.ShapeDtypeStruct((8, 128), F32),
        ],
        compiler_params=params(),
        cost_estimate=cost(40 * heads * count * tokens * HD, 9e6),
        name="attend_back",
    )(q, k, v, u, lse, delta)


def sum_kernel(pieces_ref, after_ref, out_ref):
    out_ref[...] = jnp.sum(pieces_ref[...], 0)


def sum_pieces(pieces, after):
    return pl.pallas_call(
        sum_kernel,
        out_shape=jax.ShapeDtypeStruct(pieces.shape[1:], F32),
        compiler_params=params(),
        cost_estimate=cost(pieces.size, 4 * pieces.size),
        name="sum_pieces",
    )(pieces, after)


def out_kernel(att_ref, rows_ref, own_ref, other_ref, grad_ref, keep_ref, send_ref):
    att = att_ref[0].reshape(own_ref.shape[1], att_ref.shape[3]).astype(BF16)
    term = dot(rows_ref[...], att, NT)

    @pl.when(pl.program_id(0) == 0)
    def _():
        grad_ref[...] = term

    @pl.when(pl.program_id(0) > 0)
    def _():
        grad_ref[...] += term

    send_ref[...] = dot(other_ref[...], att)
    keep_ref[...] = dot(own_ref[...], att)


def out_step(att, rows, own, other):
    _, heads, _, half = att.shape
    width, inner = own.shape
    share = rows.shape[0]
    whole = lambda a: pl.BlockSpec(a.shape, lambda i: (0, 0))
    return pl.pallas_call(
        out_kernel,
        grid=(2,),
        in_specs=[
            pl.BlockSpec((1, heads, HD, half), lambda i: (i, 0, 0, 0)),
            pl.BlockSpec((share, half), lambda i: (0, i)),
            whole(own),
            whole(other),
        ],
        out_specs=[
            pl.BlockSpec((share, inner), lambda i: (0, 0)),
            pl.BlockSpec((width, half), lambda i: (0, i)),
            pl.BlockSpec((width, half), lambda i: (0, i)),
        ],
        out_shape=[
            jax.ShapeDtypeStruct((share, inner), F32),
            jax.ShapeDtypeStruct((width, 2 * half), F32),
            jax.ShapeDtypeStruct((width, 2 * half), F32),
        ],
        compiler_params=params(),
        cost_estimate=cost(8 * half * inner * width, 12e6),
        name="project_out",
    )(att, rows, own, other)


def query_kernel(pieces_ref, norm_ref, out_ref):
    places, share, _ = out_ref.shape
    heads = places // 2
    total = jnp.sum(pieces_ref[...], 0)
    depth, half = total.shape
    rows = half // heads
    proj = (total * HD ** (-0.5)).astype(BF16)
    term = dot(norm_ref[...], proj, NT)
    for place in range(places):
        strip = place % heads * rows
        out_ref[place, :, :depth] = term[place * share : (place + 1) * share, :]
        out_ref[place, :depth, 128 : 128 + rows] = total[:, strip : strip + rows]


def query_step(pieces, norm, places):
    _, depth, half = pieces.shape
    width = norm.shape[0]
    return pl.pallas_call(
        query_kernel,
        out_shape=jax.ShapeDtypeStruct((places, width // places, 256), F32),
        compiler_params=params(),
        cost_estimate=cost(2 * half * width * depth, 6e6),
        name="query_grad",
    )(pieces, norm)


def latent_kernel(pieces_ref, qw_ref, latents_ref, cot_ref, out_ref):
    heads, depth, rows = pieces_ref.shape
    proj = pieces_ref[...].reshape(heads * depth, rows) * HD ** (-0.5)
    up = dot(proj.T.astype(BF16), qw_ref[...])
    hat, inv = layer_norm(latents_ref[...].astype(F32))
    term = norm_backward(hat, inv, up) + cot_ref[...].astype(F32) / 2
    size = out_ref.shape[2]
    for block in range(out_ref.shape[0]):
        out_ref[block] = term[:, block * size : (block + 1) * size]


def latent_step(pieces, qw, latents, cot, blocks):
    rows, width = latents.shape
    return pl.pallas_call(
        latent_kernel,
        out_shape=jax.ShapeDtypeStruct((blocks, rows, width // blocks), F32),
        compiler_params=params(),
        cost_estimate=cost(2 * rows * qw.size, 4e6),
        name="latent_grad",
    )(pieces, qw, latents, cot)


def shift(value, axis, by, side=None, minor=True):
    size = lax.axis_size(axis)
    if side is None:
        pairs = [(i, (i + by) % size) for i in range(size)]
    elif minor:
        pairs = [(i, i // side * side + (i % side + by) % side) for i in range(size)]
    else:
        pairs = [(i, (i + by * side) % size) for i in range(size)]
    return lax.ppermute(value, axis, pairs)


def pick(blocks, index):
    return lax.dynamic_index_in_dim(blocks, index, 0, False)


def scatter_sum(blocks, axis, place):
    size = blocks.shape[0]
    total = pick(blocks, place)
    for by in range(1, size):
        total = total + shift(pick(blocks, (place + by) % size), axis, by)
    return total


def relay_sum(blocks, place, cut, send):
    far = pick(blocks, (place + 2) % 4)
    front = send(far[:cut], 1)
    back = send(far[cut:], -1)
    ahead = pick(blocks, (place + 1) % 4)
    behind = pick(blocks, (place + 3) % 4)
    ahead = jnp.concatenate([ahead[:cut] + front, ahead[cut:]], 0)
    behind = jnp.concatenate([behind[:cut], behind[cut:] + back], 0)
    return pick(blocks, place) + send(ahead, 1) + send(behind, -1)


def merge_stats(stats, side, minor):
    parts = [stats] + [shift(stats, "seq", by, side, minor) for by in range(1, side)]
    top = functools.reduce(jnp.maximum, [p[0] for p in parts])
    factors = [jnp.exp(p[0] - top) for p in parts]
    total = sum(p[1] * f for p, f in zip(parts, factors))
    delta = sum(p[2] * f for p, f in zip(parts, factors))
    return jnp.stack([top, total, delta])


def local(media_tokens, latents, query_weight, key_weight, value_weight, out_weight, cotangent):
    inner = query_weight.shape[1]
    width = query_weight.shape[0]
    heads = inner // HD
    count = latents.shape[0]
    half = count // 2
    seq, tp, dp = (lax.axis_index(a) for a in ("seq", "tp", "dp"))
    seqs, tps, dps = (lax.axis_size(a) for a in ("seq", "tp", "dp"))
    side = 4
    share = width // seqs
    part = share // dps
    rows = count // seqs
    upstream = cotangent[0]
    query_turned = query_weight.T

    media_norm, latent_norm, q, k, v, u = project(
        media_tokens[0], latents, upstream, query_turned, key_weight.T, value_weight.T, out_weight
    )
    weighted, stats = forward(q, k, v, u)

    top, total, delta = merge_stats(merge_stats(stats, side, True), side, False)
    lse = top + jnp.log(total)
    delta = delta / total
    factor = (jnp.exp(stats[0] - top) / total).reshape(heads, 2, 1, half).transpose(1, 0, 2, 3)

    scaled = (weighted * factor).reshape(seqs, HD, half)
    attended_pieces = lax.all_to_all(scaled, "seq", 0, 0, tiled=True)
    dq, dk, dv, done = backward(q, k, v, u, lse, delta)

    query_pieces = lax.all_to_all(dq.reshape(seqs, HD, half), "seq", 0, 0, tiled=True)

    major, minor = seq // side, seq % side
    cut = share // 16 * 8
    along = lambda value, by: shift(value, "seq", by, side, True)
    across = lambda value, by: shift(value, "seq", by, side, False)
    key_term = dot(media_norm, dk.reshape(inner, -1), NT).reshape(side, side, share, inner)
    value_term = dot(media_norm, dv.reshape(inner, -1), NT).reshape(side, side, share, inner)
    key_rows = relay_sum(key_term.transpose(1, 0, 2, 3), minor, side // 2, along)
    value_rows = relay_sum(value_term, major, side // 2, across)
    key_rows = relay_sum(key_rows, major, cut, across)
    value_rows = relay_sum(value_rows, minor, cut, along)
    both = jnp.stack([key_rows, value_rows]).reshape(2, dps, part, inner).transpose(1, 0, 2, 3)
    grad_key, grad_value = scatter_sum(both, "dp", dp)

    attended = lax.all_gather(sum_pieces(attended_pieces, done), "seq")
    cot_cols = lax.dynamic_slice_in_dim(upstream, seq * share, share, 1).T
    own = lax.dynamic_slice_in_dim(out_weight, tp * inner, inner, 1).T
    other = lax.dynamic_slice_in_dim(out_weight, (1 - tp) * inner, inner, 1).T
    latent_cols = lax.dynamic_slice_in_dim(latents, tp * inner, inner, 1).T
    out_rows, keep, away = out_step(attended.reshape(2, heads, HD, half), cot_cols, own, other)
    arrived = lax.ppermute(away, "tp", [(0, 1), (1, 0)])
    resampled = (latent_cols.astype(F32) + (keep + arrived)).astype(BF16).T[None]
    grad_out = scatter_sum(out_rows.reshape(dps, part, inner), "dp", dp).T

    side_of = seq // heads
    norm_half = lax.dynamic_slice_in_dim(latent_norm, side_of * half, half, 1)
    sent = query_step(query_pieces, norm_half, seqs)
    sent = lax.all_to_all(sent, "seq", 0, 0, tiled=True)
    strips = lax.dynamic_slice(sent, (side_of * heads, 0, 128), (heads, HD, rows))
    latent_rows = lax.dynamic_slice_in_dim(latents, seq * rows, rows, 0)
    cot_rows = lax.dynamic_slice_in_dim(upstream, seq * rows, rows, 0)
    term = latent_step(strips, query_turned, latent_rows, cot_rows, tps * dps)
    blocks = (sent[:heads, :, :HD] + sent[heads:, :, :HD]).transpose(1, 0, 2)
    grad_query = scatter_sum(blocks.reshape(dps, part, inner), "dp", dp)
    grad_latents = jnp.sum(lax.all_to_all(term, ("tp", "dp"), 0, 0, tiled=True), 0)
    return (resampled, grad_latents, grad_query, grad_key, grad_value, grad_out)


def solution(mesh):
    placed = (
        P("dp", "seq", None),
        P(),
        P(None, "tp"),
        P(None, "tp"),
        P(None, "tp"),
        P("tp", None),
        P("dp", None, None),
    )
    return jax.shard_map(
        local,
        mesh=mesh,
        in_specs=placed,
        out_specs=(
            P("dp", None, "tp"),
            P("seq", ("tp", "dp")),
            P(("seq", "dp"), "tp"),
            P(("seq", "dp"), "tp"),
            P(("seq", "dp"), "tp"),
            P("tp", ("seq", "dp")),
        ),
        check_vma=False,
    )
```

```python
import functools

import jax
import jax.numpy as jnp
from jax import lax
from jax.experimental import pallas as pl
from jax.experimental.pallas import tpu as pltpu
from jax.sharding import PartitionSpec as P

HD = 88
VMEM = 56 * 1024 * 1024
F32 = jnp.float32
BF16 = jnp.bfloat16
NT = (((1,), (1,)), ((), ()))
TN = (((0,), (0,)), ((), ()))


def params():
    return pltpu.CompilerParams(vmem_limit_bytes=VMEM)


def cost(flops, size):
    return pl.CostEstimate(flops=int(flops), bytes_accessed=int(size), transcendentals=0)


def dot(a, b, dims=(((1,), (0,)), ((), ()))):
    return lax.dot_general(a, b, dims, preferred_element_type=F32)


def layer_norm(rows):
    average = jnp.mean(rows, -1, keepdims=True)
    centered = rows - average
    variance = jnp.mean(centered * centered, -1, keepdims=True)
    inv_std = lax.rsqrt(variance + 1e-05)
    return (centered * inv_std, inv_std)


def norm_backward(normed, inv_std, upstream):
    mean_up = jnp.mean(upstream, -1, keepdims=True)
    mean_cross = jnp.mean(upstream * normed, -1, keepdims=True)
    return inv_std * (upstream - mean_up - normed * mean_cross)


def project_kernel(
    media_ref, latents_ref, cot_ref, qw_ref, kw_ref, vw_ref, ow_ref,
    mn_ref, ln_ref, q_ref, k_ref, v_ref, u_ref,
):
    def split(ref, value):
        for head in range(ref.shape[0]):
            ref[head] = value[head * HD : (head + 1) * HD, :].astype(BF16)

    media_norm = layer_norm(media_ref[...].astype(F32))[0].T.astype(BF16)
    mn_ref[...] = media_norm
    split(k_ref, dot(kw_ref[...], media_norm))
    split(v_ref, dot(vw_ref[...], media_norm))
    latent_norm = layer_norm(latents_ref[...].astype(F32))[0].T.astype(BF16)
    ln_ref[...] = latent_norm
    split(q_ref, dot(qw_ref[...], latent_norm) * HD ** (-0.5))
    split(u_ref, dot(ow_ref[...], cot_ref[...], NT))


def project(media, latents, cot, qw, kw, vw, ow):
    tokens, width = media.shape
    count = latents.shape[0]
    inner = qw.shape[0]
    heads = inner // HD
    steps = 2
    t, c = tokens // steps, count // steps
    rows = lambda n: pl.BlockSpec((n, width), lambda i: (i, 0))
    cols = lambda n: pl.BlockSpec((width, n), lambda i: (0, i))
    whole = lambda a: pl.BlockSpec(a.shape, lambda i: (0, 0))
    turned = lambda n: pl.BlockSpec((heads, HD, n), lambda i: (0, 0, i))
    shape = jax.ShapeDtypeStruct
    return pl.pallas_call(
        project_kernel,
        grid=(steps,),
        in_specs=[rows(t), rows(c), rows(c), whole(qw), whole(kw), whole(vw), whole(ow)],
        out_specs=[cols(t), cols(c), turned(c), turned(t), turned(t), turned(c)],
        out_shape=[
            shape((width, tokens), BF16),
            shape((width, count), BF16),
            shape((heads, HD, count), BF16),
            shape((heads, HD, tokens), BF16),
            shape((heads, HD, tokens), BF16),
            shape((heads, HD, count), BF16),
        ],
        compiler_params=params(),
        cost_estimate=cost(4 * (tokens + count) * width * inner, 24e6),
        name="project",
    )(media, latents, cot, qw, kw, vw, ow)


def forward_kernel(chunk, q_ref, k_ref, v_ref, u_ref, w_ref, stat_ref):
    head = pl.program_id(0)
    count = q_ref.shape[2]
    half = count // 2
    keys = k_ref[0].astype(F32).T.astype(BF16)
    vals = v_ref[0]
    for start in range(0, count, chunk):
        cols = slice(start, start + chunk)
        scores = dot(keys, q_ref[0, :, cols])
        top = jnp.max(scores, 0, keepdims=True)
        weights = jnp.exp(scores - top)
        total = jnp.sum(weights, 0, keepdims=True)
        weighted = dot(vals, weights.astype(BF16))
        delta = jnp.sum(u_ref[0, :, cols].astype(F32) * weighted, 0, keepdims=True)
        side, inner = divmod(start, half)
        w_ref[side, 0, :, inner : inner + chunk] = weighted
        stat_ref[0, pl.ds(head, 1), cols] = top
        stat_ref[1, pl.ds(head, 1), cols] = total
        stat_ref[2, pl.ds(head, 1), cols] = delta


def forward(q, k, v, u):
    heads, _, count = q.shape
    tokens = k.shape[2]
    per_head = lambda n: pl.BlockSpec((1, HD, n), lambda h: (h, 0, 0))
    return pl.pallas_call(
        functools.partial(forward_kernel, min(256, count // 2)),
        grid=(heads,),
        in_specs=[per_head(count), per_head(tokens), per_head(tokens), per_head(count)],
        out_specs=[
            pl.BlockSpec((2, 1, HD, count // 2), lambda h: (0, h, 0, 0)),
            pl.BlockSpec((3, heads, count), lambda h: (0, 0, 0)),
        ],
        out_shape=[
            jax.ShapeDtypeStruct((2, heads, HD, count // 2), F32),
            jax.ShapeDtypeStruct((3, heads, count), F32),
        ],
        compiler_params=params(),
        cost_estimate=cost(16 * heads * count * tokens * HD, 9e6),
        name="attend",
    )(q, k, v, u)


def backward_kernel(
    chunk, q_ref, k_ref, v_ref, u_ref, stat_ref, dq_ref, dkv_ref, done_ref
):
    head = pl.program_id(0)
    count = q_ref.shape[2]
    half = count // 2
    keys_t = k_ref[0]
    keys = keys_t.astype(F32).T.astype(BF16)
    vals = v_ref[0].astype(F32).T.astype(BF16)
    key_grad = jnp.zeros(keys.shape, F32)
    value_grad = jnp.zeros(vals.shape, F32)
    total = stat_ref[1, pl.ds(head, 1), :]
    lse = stat_ref[0, pl.ds(head, 1), :] + jnp.log(total)
    delta = stat_ref[2, pl.ds(head, 1), :] / total
    for start in range(0, count, chunk):
        cols = slice(start, start + chunk)
        q = q_ref[0, :, cols]
        u = u_ref[0, :, cols]
        probs = jnp.exp(dot(keys, q) - lse[:, cols])
        grad = (probs * (dot(vals, u) - delta[:, cols])).astype(BF16)
        value_grad += dot(probs.astype(BF16), u.astype(F32).T.astype(BF16))
        key_grad += dot(grad, q.astype(F32).T.astype(BF16))
        side, inner = divmod(start, half)
        dq_ref[side, 0, :, inner : inner + chunk] = dot(keys_t, grad)
    dkv_ref[0, 0] = key_grad.T.astype(BF16)
    dkv_ref[1, 0] = value_grad.T.astype(BF16)
    done_ref[...] = jnp.zeros_like(done_ref)


def backward(q, k, v, u, stats):
    heads, _, count = q.shape
    tokens = k.shape[2]
    per_head = lambda n: pl.BlockSpec((1, HD, n), lambda h: (h, 0, 0))
    return pl.pallas_call(
        functools.partial(backward_kernel, min(256, count // 2)),
        grid=(heads,),
        in_specs=[
            per_head(count), per_head(tokens), per_head(tokens), per_head(count),
            pl.BlockSpec((3, heads, count), lambda h: (0, 0, 0)),
        ],
        out_specs=[
            pl.BlockSpec((2, 1, HD, count // 2), lambda h: (0, h, 0, 0)),
            pl.BlockSpec((2, 1, HD, tokens), lambda h: (0, h, 0, 0)),
            pl.BlockSpec((8, 128), lambda h: (0, 0)),
        ],
        out_shape=[
            jax.ShapeDtypeStruct((2, heads, HD, count // 2), F32),
            jax.ShapeDtypeStruct((2, heads, HD, tokens), BF16),
            jax.ShapeDtypeStruct((8, 128), F32),
        ],
        compiler_params=params(),
        cost_estimate=cost(40 * heads * count * tokens * HD, 9e6),
        name="attend_back",
    )(q, k, v, u, stats)


def sum_kernel(pieces_ref, after_ref, out_ref):
    out_ref[...] = jnp.sum(pieces_ref[...], 0)


def sum_pieces(pieces, after):
    return pl.pallas_call(
        sum_kernel,
        out_shape=jax.ShapeDtypeStruct(pieces.shape[1:], F32),
        compiler_params=params(),
        cost_estimate=cost(pieces.size, 4 * pieces.size),
        name="sum_pieces",
    )(pieces, after)


def out_kernel(att_ref, rows_ref, own_ref, other_ref, grad_ref, keep_ref, send_ref):
    att = att_ref[0].reshape(own_ref.shape[1], att_ref.shape[3]).astype(BF16)
    term = dot(rows_ref[...], att, NT)

    @pl.when(pl.program_id(0) == 0)
    def _():
        grad_ref[...] = term

    @pl.when(pl.program_id(0) > 0)
    def _():
        grad_ref[...] += term

    send_ref[...] = dot(other_ref[...], att)
    keep_ref[...] = dot(own_ref[...], att)


def out_step(att, rows, own, other):
    _, heads, _, half = att.shape
    width, inner = own.shape
    share = rows.shape[0]
    whole = lambda a: pl.BlockSpec(a.shape, lambda i: (0, 0))
    return pl.pallas_call(
        out_kernel,
        grid=(2,),
        in_specs=[
            pl.BlockSpec((1, heads, HD, half), lambda i: (i, 0, 0, 0)),
            pl.BlockSpec((share, half), lambda i: (0, i)),
            whole(own),
            whole(other),
        ],
        out_specs=[
            pl.BlockSpec((share, inner), lambda i: (0, 0)),
            pl.BlockSpec((width, half), lambda i: (0, i)),
            pl.BlockSpec((width, half), lambda i: (0, i)),
        ],
        out_shape=[
            jax.ShapeDtypeStruct((share, inner), F32),
            jax.ShapeDtypeStruct((width, 2 * half), F32),
            jax.ShapeDtypeStruct((width, 2 * half), F32),
        ],
        compiler_params=params(),
        cost_estimate=cost(8 * half * inner * width, 12e6),
        name="project_out",
    )(att, rows, own, other)


def query_kernel(pieces_ref, norm_ref, out_ref):
    places, share, _ = out_ref.shape
    heads = places // 2
    total = jnp.sum(pieces_ref[...], 0)
    depth, half = total.shape
    rows = half // heads
    proj = (total * HD ** (-0.5)).astype(BF16)
    term = dot(norm_ref[...], proj, NT)
    for place in range(places):
        strip = place % heads * rows
        out_ref[place, :, :depth] = term[place * share : (place + 1) * share, :]
        out_ref[place, :depth, 128 : 128 + rows] = total[:, strip : strip + rows]


def query_step(pieces, norm, places):
    _, depth, half = pieces.shape
    width = norm.shape[0]
    return pl.pallas_call(
        query_kernel,
        out_shape=jax.ShapeDtypeStruct((places, width // places, 256), F32),
        compiler_params=params(),
        cost_estimate=cost(2 * half * width * depth, 6e6),
        name="query_grad",
    )(pieces, norm)


def latent_kernel(pieces_ref, qw_ref, latents_ref, cot_ref, out_ref):
    heads, depth, rows = pieces_ref.shape
    proj = pieces_ref[...].reshape(heads * depth, rows) * HD ** (-0.5)
    up = dot(proj.T.astype(BF16), qw_ref[...])
    hat, inv = layer_norm(latents_ref[...].astype(F32))
    term = norm_backward(hat, inv, up) + cot_ref[...].astype(F32) / 2
    size = out_ref.shape[2]
    for block in range(out_ref.shape[0]):
        out_ref[block] = term[:, block * size : (block + 1) * size]


def latent_step(pieces, qw, latents, cot, blocks):
    rows, width = latents.shape
    return pl.pallas_call(
        latent_kernel,
        out_shape=jax.ShapeDtypeStruct((blocks, rows, width // blocks), F32),
        compiler_params=params(),
        cost_estimate=cost(2 * rows * qw.size, 4e6),
        name="latent_grad",
    )(pieces, qw, latents, cot)


def shift(value, axis, by, side=None, minor=True):
    size = lax.axis_size(axis)
    if side is None:
        pairs = [(i, (i + by) % size) for i in range(size)]
    elif minor:
        pairs = [(i, i // side * side + (i % side + by) % side) for i in range(size)]
    else:
        pairs = [(i, (i + by * side) % size) for i in range(size)]
    return lax.ppermute(value, axis, pairs)


def pick(blocks, index):
    return lax.dynamic_index_in_dim(blocks, index, 0, False)


def scatter_sum(blocks, axis, place):
    size = blocks.shape[0]
    total = pick(blocks, place)
    for by in range(1, size):
        total = total + shift(pick(blocks, (place + by) % size), axis, by)
    return total


def relay_sum(blocks, place, cut, send):
    far = pick(blocks, (place + 2) % 4)
    front = send(far[:cut], 1)
    back = send(far[cut:], -1)
    ahead = pick(blocks, (place + 1) % 4)
    behind = pick(blocks, (place + 3) % 4)
    ahead = jnp.concatenate([ahead[:cut] + front, ahead[cut:]], 0)
    behind = jnp.concatenate([behind[:cut], behind[cut:] + back], 0)
    return pick(blocks, place) + send(ahead, 1) + send(behind, -1)


def merge_stats(stats, side, minor):
    parts = [stats] + [shift(stats, "seq", by, side, minor) for by in range(1, side)]
    top = functools.reduce(jnp.maximum, [p[0] for p in parts])
    factors = [jnp.exp(p[0] - top) for p in parts]
    total = sum(p[1] * f for p, f in zip(parts, factors))
    delta = sum(p[2] * f for p, f in zip(parts, factors))
    return jnp.stack([top, total, delta])


def local(media_tokens, latents, query_weight, key_weight, value_weight, out_weight, cotangent):
    inner = query_weight.shape[1]
    width = query_weight.shape[0]
    heads = inner // HD
    count = latents.shape[0]
    half = count // 2
    seq, tp, dp = (lax.axis_index(a) for a in ("seq", "tp", "dp"))
    seqs, tps, dps = (lax.axis_size(a) for a in ("seq", "tp", "dp"))
    side = 4
    share = width // seqs
    part = share // dps
    padded = -(-part // 8) * 8
    rows = count // seqs
    upstream = cotangent[0]
    query_turned = query_weight.T

    media_norm, latent_norm, q, k, v, u = project(
        media_tokens[0], latents, upstream, query_turned, key_weight.T, value_weight.T, out_weight
    )
    weighted, stats = forward(q, k, v, u)

    whole = merge_stats(merge_stats(stats, side, True), side, False)
    factor = (jnp.exp(stats[0] - whole[0]) / whole[1]).reshape(heads, 2, 1, half).transpose(1, 0, 2, 3)

    scaled = (weighted * factor).reshape(seqs, HD, half)
    attended_pieces = lax.all_to_all(scaled, "seq", 0, 0, tiled=True)
    dq, dkv, done = backward(q, k, v, u, whole)
    seq, tp, done = lax.optimization_barrier((seq, tp, done))

    query_pieces = lax.all_to_all(dq.reshape(seqs, HD, half), "seq", 0, 0, tiled=True)

    blocks = media_norm.reshape(seqs, dps, part, -1).transpose(1, 0, 2, 3)
    blocks = jnp.pad(blocks, ((0, 0), (0, 0), (0, padded - part), (0, 0)))
    term = dot(blocks.reshape(dps * seqs * padded, -1), dkv.reshape(2 * inner, -1), NT)
    term = term.reshape(dps, seqs * padded, 2 * inner)
    term = relay_sum(term, dp, seqs * padded // 2, lambda value, by: shift(value, "dp", by))
    term = lax.all_to_all(term.reshape(seqs, padded, 2 * inner), "seq", 0, 0, tiled=True)
    term = jnp.sum(term, 0)[:part]
    grad_key, grad_value = term[:, :inner], term[:, inner:]

    attended = lax.all_gather(sum_pieces(attended_pieces, done), "seq")
    cot_cols = lax.dynamic_slice_in_dim(upstream, seq * share, share, 1).T
    own = lax.dynamic_slice_in_dim(out_weight, tp * inner, inner, 1).T
    other = lax.dynamic_slice_in_dim(out_weight, (1 - tp) * inner, inner, 1).T
    latent_cols = lax.dynamic_slice_in_dim(latents, tp * inner, inner, 1).T
    out_rows, keep, away = out_step(attended.reshape(2, heads, HD, half), cot_cols, own, other)
    arrived = lax.ppermute(away, "tp", [(0, 1), (1, 0)])
    resampled = (latent_cols.astype(F32) + (keep + arrived)).astype(BF16).T[None]
    grad_out = scatter_sum(out_rows.reshape(dps, part, inner), "dp", dp).T

    side_of = seq // heads
    norm_half = lax.dynamic_slice_in_dim(latent_norm, side_of * half, half, 1)
    sent = query_step(query_pieces, norm_half, seqs)
    sent = lax.all_to_all(sent, "seq", 0, 0, tiled=True)
    strips = lax.dynamic_slice(sent, (side_of * heads, 0, 128), (heads, HD, rows))
    latent_rows = lax.dynamic_slice_in_dim(latents, seq * rows, rows, 0)
    cot_rows = lax.dynamic_slice_in_dim(upstream, seq * rows, rows, 0)
    term = latent_step(strips, query_turned, latent_rows, cot_rows, tps * dps)
    blocks = (sent[:heads, :, :HD] + sent[heads:, :, :HD]).transpose(1, 0, 2)
    grad_query = scatter_sum(blocks.reshape(dps, part, inner), "dp", dp)
    grad_latents = jnp.sum(lax.all_to_all(term, ("tp", "dp"), 0, 0, tiled=True), 0)
    return (resampled, grad_latents, grad_query, grad_key, grad_value, grad_out)


def solution(mesh):
    placed = (
        P("dp", "seq", None),
        P(),
        P(None, "tp"),
        P(None, "tp"),
        P(None, "tp"),
        P("tp", None),
        P("dp", None, None),
    )
    return jax.shard_map(
        local,
        mesh=mesh,
        in_specs=placed,
        out_specs=(
            P("dp", None, "tp"),
            P("seq", ("tp", "dp")),
            P(("seq", "dp"), "tp"),
            P(("seq", "dp"), "tp"),
            P(("seq", "dp"), "tp"),
            P("tp", ("seq", "dp")),
        ),
        check_vma=False,
    )
```

```python
import functools

import jax
import jax.numpy as jnp
from jax import lax
from jax.experimental import pallas as pl
from jax.experimental.pallas import tpu as pltpu
from jax.sharding import PartitionSpec as P

HD = 88
VMEM = 56 * 1024 * 1024
F32 = jnp.float32
BF16 = jnp.bfloat16
NT = (((1,), (1,)), ((), ()))
TN = (((0,), (0,)), ((), ()))


def params():
    return pltpu.CompilerParams(vmem_limit_bytes=VMEM)


def cost(flops, size):
    return pl.CostEstimate(flops=int(flops), bytes_accessed=int(size), transcendentals=0)


def dot(a, b, dims=(((1,), (0,)), ((), ()))):
    return lax.dot_general(a, b, dims, preferred_element_type=F32)


def layer_norm(rows):
    average = jnp.mean(rows, -1, keepdims=True)
    centered = rows - average
    variance = jnp.mean(centered * centered, -1, keepdims=True)
    inv_std = lax.rsqrt(variance + 1e-05)
    return (centered * inv_std, inv_std)


def norm_backward(normed, inv_std, upstream):
    mean_up = jnp.mean(upstream, -1, keepdims=True)
    mean_cross = jnp.mean(upstream * normed, -1, keepdims=True)
    return inv_std * (upstream - mean_up - normed * mean_cross)


def project_kernel(media, kw, vw, latents, qw, cot, ow, mn, ln, k, v, q, u, *scratch):
    arrays = [media, kw, vw, latents, qw, cot, ow, mn, ln, k, v, q, u]
    held, (arrive, leave) = scratch[: len(arrays)], scratch[len(arrays) :]
    media_at, kw_at, vw_at, latents_at, qw_at, cot_at, ow_at, mn_at, ln_at, k_at, v_at, q_at, u_at = held
    fetch = [pltpu.make_async_copy(arrays[i], held[i], arrive.at[i]) for i in range(7)]
    store = [pltpu.make_async_copy(held[7 + i], arrays[7 + i], leave.at[i]) for i in range(6)]
    for copy in fetch:
        copy.start()

    def chunks(count):
        size = min(256, count)
        return [slice(i, i + size) for i in range(0, count, size)]

    def normalise(source, target):
        for rows in chunks(source.shape[0]):
            target[:, rows] = layer_norm(source[rows, :].astype(F32))[0].T.astype(BF16)

    def split(target, cols, value):
        for head in range(target.shape[0]):
            target[head, :, cols] = value[head * HD : (head + 1) * HD, :].astype(BF16)

    fetch[0].wait()
    normalise(media_at, mn_at)
    store[0].start()
    for i, weight, target in ((1, kw_at, k_at), (2, vw_at, v_at)):
        fetch[i].wait()
        for cols in chunks(mn_at.shape[1]):
            split(target, cols, dot(weight[...], mn_at[:, cols]))
        store[1 + i].start()
    fetch[3].wait()
    normalise(latents_at, ln_at)
    store[1].start()
    fetch[4].wait()
    for cols in chunks(ln_at.shape[1]):
        split(q_at, cols, dot(qw_at[...], ln_at[:, cols]) * HD ** (-0.5))
    store[4].start()
    fetch[5].wait()
    fetch[6].wait()
    for rows in chunks(cot_at.shape[0]):
        split(u_at, rows, dot(ow_at[...], cot_at[rows, :], NT))
    store[5].start()
    for copy in store:
        copy.wait()


def project(media, latents, cot, qw, kw, vw, ow):
    tokens, width = media.shape
    count = latents.shape[0]
    inner = qw.shape[0]
    heads = inner // HD
    ins = (media, kw, vw, latents, qw, cot, ow)
    outs = [
        jax.ShapeDtypeStruct(size, BF16)
        for size in (
            (width, tokens), (width, count),
            (heads, HD, tokens), (heads, HD, tokens), (heads, HD, count), (heads, HD, count),
        )
    ]
    anywhere = pl.BlockSpec(memory_space=pl.ANY)
    return pl.pallas_call(
        project_kernel,
        in_specs=[anywhere] * len(ins),
        out_specs=[anywhere] * len(outs),
        out_shape=outs,
        scratch_shapes=[pltpu.VMEM(a.shape, BF16) for a in (*ins, *outs)]
        + [pltpu.SemaphoreType.DMA((len(ins),)), pltpu.SemaphoreType.DMA((len(outs),))],
        compiler_params=params(),
        cost_estimate=cost(4 * (tokens + count) * width * inner, 24e6),
        name="project",
    )(*ins)


def forward_kernel(chunk, q_ref, k_ref, v_ref, u_ref, w_ref, stat_ref):
    step = pl.program_id(0)
    group, _, count = q_ref.shape
    half = count // 2

    def attend(limits):
        for item in range(group):
            head = step * group + item
            keys = k_ref[item].astype(F32).T.astype(BF16)
            vals = v_ref[item]
            for start in range(0, count, chunk):
                cols = slice(start, start + chunk)
                scores = dot(keys, q_ref[item, :, cols])
                if limits is None:
                    top = jnp.max(scores, 0, keepdims=True)
                else:
                    top = limits[item][:, cols]
                weights = jnp.exp(scores - top)
                total = jnp.sum(weights, 0, keepdims=True)
                weighted = dot(vals, weights.astype(BF16))
                delta = jnp.sum(u_ref[item, :, cols].astype(F32) * weighted, 0, keepdims=True)
                side, inner = divmod(start, half)
                w_ref[side, item, :, inner : inner + chunk] = weighted
                stat_ref[0, pl.ds(head, 1), cols] = top
                stat_ref[1, pl.ds(head, 1), cols] = total
                stat_ref[2, pl.ds(head, 1), cols] = delta

    limits = []
    for item in range(group):
        q, k = q_ref[item].astype(F32), k_ref[item].astype(F32)
        longest = jnp.max(jnp.sum(k * k, 0, keepdims=True), 1, keepdims=True)
        limits.append(jnp.sqrt(jnp.sum(q * q, 0, keepdims=True) * longest) * 1.0001)
    highest = functools.reduce(jnp.maximum, [jnp.max(limit) for limit in limits])

    @pl.when(highest < 32.0)
    def _():
        attend(limits)

    @pl.when(jnp.logical_not(highest < 32.0))
    def _():
        attend(None)


def forward(q, k, v, u):
    heads, _, count = q.shape
    tokens = k.shape[2]
    group = 2
    per_head = lambda n: pl.BlockSpec((group, HD, n), lambda h: (h, 0, 0))
    return pl.pallas_call(
        functools.partial(forward_kernel, min(256, count // 2)),
        grid=(heads // group,),
        in_specs=[per_head(count), per_head(tokens), per_head(tokens), per_head(count)],
        out_specs=[
            pl.BlockSpec((2, group, HD, count // 2), lambda h: (0, h, 0, 0)),
            pl.BlockSpec((3, heads, count), lambda h: (0, 0, 0)),
        ],
        out_shape=[
            jax.ShapeDtypeStruct((2, heads, HD, count // 2), F32),
            jax.ShapeDtypeStruct((3, heads, count), F32),
        ],
        compiler_params=params(),
        cost_estimate=cost(16 * heads * count * tokens * HD, 9e6),
        name="attend",
    )(q, k, v, u)


def backward_kernel(
    chunk, q_ref, k_ref, v_ref, u_ref, stat_ref, dq_ref, dkv_ref, done_ref
):
    group, _, count = q_ref.shape
    half = count // 2
    for item in range(group):
        head = pl.program_id(0) * group + item
        keys_t = k_ref[item]
        keys = keys_t.astype(F32).T.astype(BF16)
        vals = v_ref[item].astype(F32).T.astype(BF16)
        key_grad = jnp.zeros(keys.shape, F32)
        value_grad = jnp.zeros(vals.shape, F32)
        total = stat_ref[1, pl.ds(head, 1), :]
        lse = stat_ref[0, pl.ds(head, 1), :] + jnp.log(total)
        delta = stat_ref[2, pl.ds(head, 1), :] / total
        for start in range(0, count, chunk):
            cols = slice(start, start + chunk)
            q = q_ref[item, :, cols]
            u = u_ref[item, :, cols]
            probs = jnp.exp(dot(keys, q) - lse[:, cols])
            grad = (probs * (dot(vals, u) - delta[:, cols])).astype(BF16)
            value_grad += dot(probs.astype(BF16), u.astype(F32).T.astype(BF16))
            key_grad += dot(grad, q.astype(F32).T.astype(BF16))
            side, inner = divmod(start, half)
            dq_ref[side, item, :, inner : inner + chunk] = dot(keys_t, grad)
        dkv_ref[0, item] = key_grad.T.astype(BF16)
        dkv_ref[1, item] = value_grad.T.astype(BF16)
    done_ref[...] = jnp.zeros_like(done_ref)


def backward(q, k, v, u, stats):
    heads, _, count = q.shape
    tokens = k.shape[2]
    group = 2
    per_head = lambda n: pl.BlockSpec((group, HD, n), lambda h: (h, 0, 0))
    return pl.pallas_call(
        functools.partial(backward_kernel, min(256, count // 2)),
        grid=(heads // group,),
        in_specs=[
            per_head(count), per_head(tokens), per_head(tokens), per_head(count),
            pl.BlockSpec((3, heads, count), lambda h: (0, 0, 0)),
        ],
        out_specs=[
            pl.BlockSpec((2, group, HD, count // 2), lambda h: (0, h, 0, 0)),
            pl.BlockSpec((2, group, HD, tokens), lambda h: (0, h, 0, 0)),
            pl.BlockSpec((8, 128), lambda h: (0, 0)),
        ],
        out_shape=[
            jax.ShapeDtypeStruct((2, heads, HD, count // 2), F32),
            jax.ShapeDtypeStruct((2, heads, HD, tokens), BF16),
            jax.ShapeDtypeStruct((8, 128), F32),
        ],
        compiler_params=params(),
        cost_estimate=cost(40 * heads * count * tokens * HD, 9e6),
        name="attend_back",
    )(q, k, v, u, stats)


def sum_kernel(pieces_ref, *refs):
    refs[-1][...] = jnp.sum(pieces_ref[...], 0)


def sum_pieces(pieces, *after):
    return pl.pallas_call(
        sum_kernel,
        in_specs=[pl.BlockSpec(memory_space=pltpu.VMEM)] + [pl.BlockSpec(memory_space=pl.ANY)] * len(after),
        out_shape=jax.ShapeDtypeStruct(pieces.shape[1:], F32),
        compiler_params=params(),
        cost_estimate=cost(pieces.size, 4 * pieces.size),
        name="sum_pieces",
    )(pieces, *after)


def out_kernel(att_ref, rows_ref, own_ref, other_ref, after_ref, grad_ref, keep_ref, send_ref):
    att = att_ref[0].reshape(own_ref.shape[1], att_ref.shape[3]).astype(BF16)
    term = dot(rows_ref[...], att, NT)

    @pl.when(pl.program_id(0) == 0)
    def _():
        grad_ref[...] = term

    @pl.when(pl.program_id(0) > 0)
    def _():
        grad_ref[...] += term

    send_ref[...] = dot(other_ref[...], att)
    keep_ref[...] = dot(own_ref[...], att)


def out_step(att, rows, own, other, after):
    _, heads, _, half = att.shape
    width, inner = own.shape
    share = rows.shape[0]
    whole = lambda a: pl.BlockSpec(a.shape, lambda i: (0, 0))
    return pl.pallas_call(
        out_kernel,
        grid=(2,),
        in_specs=[
            pl.BlockSpec((1, heads, HD, half), lambda i: (i, 0, 0, 0)),
            pl.BlockSpec((share, half), lambda i: (0, i)),
            whole(own),
            whole(other),
            pl.BlockSpec(memory_space=pl.ANY),
        ],
        out_specs=[
            pl.BlockSpec((share, inner), lambda i: (0, 0)),
            pl.BlockSpec((width, half), lambda i: (0, i)),
            pl.BlockSpec((width, half), lambda i: (0, i)),
        ],
        out_shape=[
            jax.ShapeDtypeStruct((share, inner), F32),
            jax.ShapeDtypeStruct((width, 2 * half), F32),
            jax.ShapeDtypeStruct((width, 2 * half), F32),
        ],
        compiler_params=params(),
        cost_estimate=cost(8 * half * inner * width, 12e6),
        name="project_out",
    )(att, rows, own, other, after)


def query_kernel(pieces_ref, norm_ref, out_ref):
    places, share, _ = out_ref.shape
    heads = places // 2
    total = jnp.sum(pieces_ref[...], 0)
    depth, half = total.shape
    rows = half // heads
    proj = (total * HD ** (-0.5)).astype(BF16)
    term = dot(norm_ref[...], proj, NT)
    for place in range(places):
        strip = place % heads * rows
        out_ref[place, :, :depth] = term[place * share : (place + 1) * share, :]
        out_ref[place, :depth, 128 : 128 + rows] = total[:, strip : strip + rows]


def query_step(pieces, norm, places):
    _, depth, half = pieces.shape
    width = norm.shape[0]
    return pl.pallas_call(
        query_kernel,
        out_shape=jax.ShapeDtypeStruct((places, width // places, 256), F32),
        compiler_params=params(),
        cost_estimate=cost(2 * half * width * depth, 6e6),
        name="query_grad",
    )(pieces, norm)


def latent_kernel(pieces_ref, qw_ref, latents_ref, cot_ref, out_ref):
    heads, depth, rows = pieces_ref.shape
    proj = pieces_ref[...].reshape(heads * depth, rows) * HD ** (-0.5)
    up = dot(proj.T.astype(BF16), qw_ref[...])
    hat, inv = layer_norm(latents_ref[...].astype(F32))
    term = norm_backward(hat, inv, up) + cot_ref[...].astype(F32) / 2
    size = out_ref.shape[2]
    for block in range(out_ref.shape[0]):
        out_ref[block] = term[:, block * size : (block + 1) * size]


def latent_step(pieces, qw, latents, cot, blocks):
    rows, width = latents.shape
    return pl.pallas_call(
        latent_kernel,
        out_shape=jax.ShapeDtypeStruct((blocks, rows, width // blocks), F32),
        compiler_params=params(),
        cost_estimate=cost(2 * rows * qw.size, 4e6),
        name="latent_grad",
    )(pieces, qw, latents, cot)


def shift(value, axis, by, side=None, minor=True):
    size = lax.axis_size(axis)
    if side is None:
        pairs = [(i, (i + by) % size) for i in range(size)]
    elif minor:
        pairs = [(i, i // side * side + (i % side + by) % side) for i in range(size)]
    else:
        pairs = [(i, (i + by * side) % size) for i in range(size)]
    return lax.ppermute(value, axis, pairs)


def pick(blocks, index):
    return lax.dynamic_index_in_dim(blocks, index, 0, False)


def scatter_sum(blocks, axis, place, side=None, minor=True):
    size = blocks.shape[0]
    total = pick(blocks, place)
    for by in range(1, size):
        total = total + shift(pick(blocks, (place + by) % size), axis, by, side, minor)
    return total


def relay_start(blocks, place, cut, send):
    far = pick(blocks, (place + 2) % 4)
    return send(far[:cut], 1), send(far[cut:], -1)


def relay_end(blocks, place, cut, send, front, back):
    ahead = pick(blocks, (place + 1) % 4)
    behind = pick(blocks, (place + 3) % 4)
    ahead = jnp.concatenate([ahead[:cut] + front, ahead[cut:]], 0)
    behind = jnp.concatenate([behind[:cut], behind[cut:] + back], 0)
    return pick(blocks, place) + send(ahead, 1) + send(behind, -1)


def merge_stats(stats, side, minor):
    parts = [stats] + [shift(stats, "seq", by, side, minor) for by in range(1, side)]
    top = functools.reduce(jnp.maximum, [p[0] for p in parts])
    factors = [jnp.exp(p[0] - top) for p in parts]
    total = sum(p[1] * f for p, f in zip(parts, factors))
    delta = sum(p[2] * f for p, f in zip(parts, factors))
    return jnp.stack([top, total, delta])


def local(media_tokens, latents, query_weight, key_weight, value_weight, out_weight, cotangent):
    inner = query_weight.shape[1]
    width = query_weight.shape[0]
    heads = inner // HD
    count = latents.shape[0]
    half = count // 2
    seq, tp, dp = (lax.axis_index(a) for a in ("seq", "tp", "dp"))
    seqs, tps, dps = (lax.axis_size(a) for a in ("seq", "tp", "dp"))
    side = 4
    share = width // seqs
    part = share // dps
    padded = -(-part // 8) * 8
    rows = count // seqs
    upstream = cotangent[0]
    query_turned = query_weight.T

    media_norm, latent_norm, k, v, q, u = project(
        media_tokens[0], latents, upstream, query_turned, key_weight.T, value_weight.T, out_weight
    )
    weighted, stats = forward(q, k, v, u)

    whole = merge_stats(merge_stats(stats, side, True), side, False)
    factor = (jnp.exp(stats[0] - whole[0]) / whole[1]).reshape(heads, 2, 1, half).transpose(1, 0, 2, 3)

    scaled = (weighted * factor).reshape(seqs, HD, half)
    attended_pieces = lax.all_to_all(scaled, "seq", 0, 0, tiled=True)
    dq, dkv, done = backward(q, k, v, u, whole)
    seq, tp, done = lax.optimization_barrier((seq, tp, done))

    query_pieces = lax.all_to_all(dq.reshape(seqs, HD, half), "seq", 0, 0, tiled=True)

    major, minor = seq // side, seq % side
    blocks = media_norm.reshape(seqs, dps, part, -1).transpose(1, 0, 2, 3)
    blocks = jnp.pad(blocks, ((0, 0), (0, 0), (0, padded - part), (0, 0)))
    blocks = blocks.reshape(dps * seqs * padded, -1)
    grads = dkv.reshape(2 * inner, -1)
    split = (inner // 128 + 1) * 128
    terms = [dot(blocks, grads[:split], NT), dot(blocks, grads[split:], NT)]
    terms = [t.reshape(dps, seqs * padded, -1) for t in terms]
    ring = (dp, seqs * padded // 2, lambda value, by: shift(value, "dp", by))
    halves = [relay_start(t, *ring) for t in terms]
    attended = sum_pieces(attended_pieces, terms[1], *halves[0])
    terms = [relay_end(t, *ring, *h) for t, h in zip(terms, halves)]
    first, second = (t.reshape(side, side, padded, -1) for t in terms)
    first = scatter_sum(first.transpose(1, 0, 2, 3), "seq", minor, side, True)
    first = scatter_sum(first, "seq", major, side, False)
    second = scatter_sum(second, "seq", major, side, False)
    second = scatter_sum(second, "seq", minor, side, True)
    grad_key = first[:part, :inner]
    grad_value = jnp.concatenate([first[:part, inner:], second[:part]], 1)

    side_of = seq // heads
    norm_half = lax.dynamic_slice_in_dim(latent_norm, side_of * half, half, 1)
    term = query_step(query_pieces, norm_half, seqs)
    sent = lax.all_to_all(term, "seq", 0, 0, tiled=True)
    strips = lax.dynamic_slice(sent, (side_of * heads, 0, 128), (heads, HD, rows))
    latent_rows = lax.dynamic_slice_in_dim(latents, seq * rows, rows, 0)
    cot_rows = lax.dynamic_slice_in_dim(upstream, seq * rows, rows, 0)
    back = latent_step(strips, query_turned, latent_rows, cot_rows, tps * dps)
    blocks = (sent[:heads, :, :HD] + sent[heads:, :, :HD]).transpose(1, 0, 2)
    grad_query = scatter_sum(blocks.reshape(dps, part, inner), "dp", dp)
    grad_latents = jnp.sum(lax.all_to_all(back, ("tp", "dp"), 0, 0, tiled=True), 0)

    attended = lax.all_gather(attended, "seq")
    cot_cols = lax.dynamic_slice_in_dim(upstream, seq * share, share, 1).T
    own = lax.dynamic_slice_in_dim(out_weight, tp * inner, inner, 1).T
    other = lax.dynamic_slice_in_dim(out_weight, (1 - tp) * inner, inner, 1).T
    latent_cols = lax.dynamic_slice_in_dim(latents, tp * inner, inner, 1).T
    out_rows, keep, away = out_step(
        attended.reshape(2, heads, HD, half), cot_cols, own, other, term
    )
    arrived = lax.ppermute(away, "tp", [(0, 1), (1, 0)])
    resampled = (latent_cols.astype(F32) + (keep + arrived)).astype(BF16).T[None]
    grad_out = scatter_sum(out_rows.reshape(dps, part, inner), "dp", dp).T

    return (resampled, grad_latents, grad_query, grad_key, grad_value, grad_out)


def solution(mesh):
    placed = (
        P("dp", "seq", None),
        P(),
        P(None, "tp"),
        P(None, "tp"),
        P(None, "tp"),
        P("tp", None),
        P("dp", None, None),
    )
    return jax.shard_map(
        local,
        mesh=mesh,
        in_specs=placed,
        out_specs=(
            P("dp", None, "tp"),
            P("seq", ("tp", "dp")),
            P(("seq", "dp"), "tp"),
            P(("seq", "dp"), "tp"),
            P(("seq", "dp"), "tp"),
            P("tp", ("seq", "dp")),
        ),
        check_vma=False,
    )
```

```python
import functools

import jax
import jax.numpy as jnp
from jax import lax
from jax.experimental import pallas as pl
from jax.experimental.pallas import tpu as pltpu
from jax.sharding import PartitionSpec as P

HD = 88
VMEM = 56 * 1024 * 1024
F32 = jnp.float32
BF16 = jnp.bfloat16
NT = (((1,), (1,)), ((), ()))
TN = (((0,), (0,)), ((), ()))


def params():
    return pltpu.CompilerParams(vmem_limit_bytes=VMEM)


def cost(flops, size):
    return pl.CostEstimate(flops=int(flops), bytes_accessed=int(size), transcendentals=0)


def dot(a, b, dims=(((1,), (0,)), ((), ()))):
    return lax.dot_general(a, b, dims, preferred_element_type=F32)


def layer_norm(rows):
    average = jnp.mean(rows, -1, keepdims=True)
    centered = rows - average
    variance = jnp.mean(centered * centered, -1, keepdims=True)
    inv_std = lax.rsqrt(variance + 1e-05)
    return (centered * inv_std, inv_std)


def norm_backward(normed, inv_std, upstream):
    mean_up = jnp.mean(upstream, -1, keepdims=True)
    mean_cross = jnp.mean(upstream * normed, -1, keepdims=True)
    return inv_std * (upstream - mean_up - normed * mean_cross)


def project_kernel(media, kw, vw, latents, qw, cot, ow, mn, ln, k, v, q, u, *scratch):
    arrays = [media, kw, vw, latents, qw, cot, ow, mn, ln, k, v, q, u]
    held, (arrive, leave) = scratch[: len(arrays)], scratch[len(arrays) :]
    media_at, kw_at, vw_at, latents_at, qw_at, cot_at, ow_at, mn_at, ln_at, k_at, v_at, q_at, u_at = held
    fetch = [pltpu.make_async_copy(arrays[i], held[i], arrive.at[i]) for i in range(7)]
    store = [pltpu.make_async_copy(held[7 + i], arrays[7 + i], leave.at[i]) for i in range(6)]
    for copy in fetch:
        copy.start()

    def chunks(count, body):
        size = min(256, count)

        @pl.loop(0, count // size)
        def _(i):
            body(pl.ds(pl.multiple_of(i * size, size), size))

    def normalise(source, target):
        def body(rows):
            target[:, rows] = layer_norm(source[rows, :].astype(F32))[0].T.astype(BF16)

        chunks(source.shape[0], body)

    def split(target, cols, value):
        for head in range(target.shape[0]):
            target[head, :, cols] = value[head * HD : (head + 1) * HD, :].astype(BF16)

    fetch[0].wait()
    normalise(media_at, mn_at)
    store[0].start()
    for i, weight, target in ((1, kw_at, k_at), (2, vw_at, v_at)):
        fetch[i].wait()
        chunks(
            mn_at.shape[1],
            lambda cols: split(target, cols, dot(weight[...], mn_at[:, cols])),
        )
        store[1 + i].start()
    fetch[3].wait()
    normalise(latents_at, ln_at)
    store[1].start()
    fetch[4].wait()
    chunks(
        ln_at.shape[1],
        lambda cols: split(q_at, cols, dot(qw_at[...], ln_at[:, cols]) * HD ** (-0.5)),
    )
    store[4].start()
    fetch[5].wait()
    fetch[6].wait()
    chunks(
        cot_at.shape[0],
        lambda rows: split(u_at, rows, dot(ow_at[...], cot_at[rows, :], NT)),
    )
    store[5].start()
    for copy in store:
        copy.wait()


def project(media, latents, cot, qw, kw, vw, ow):
    tokens, width = media.shape
    count = latents.shape[0]
    inner = qw.shape[0]
    heads = inner // HD
    ins = (media, kw, vw, latents, qw, cot, ow)
    outs = [
        jax.ShapeDtypeStruct(size, BF16)
        for size in (
            (width, tokens), (width, count),
            (heads, HD, tokens), (heads, HD, tokens), (heads, HD, count), (heads, HD, count),
        )
    ]
    anywhere = pl.BlockSpec(memory_space=pl.ANY)
    return pl.pallas_call(
        project_kernel,
        in_specs=[anywhere] * len(ins),
        out_specs=[anywhere] * len(outs),
        out_shape=outs,
        scratch_shapes=[pltpu.VMEM(a.shape, BF16) for a in (*ins, *outs)]
        + [pltpu.SemaphoreType.DMA((len(ins),)), pltpu.SemaphoreType.DMA((len(outs),))],
        compiler_params=params(),
        cost_estimate=cost(4 * (tokens + count) * width * inner, 24e6),
        name="project",
    )(*ins)


def forward_kernel(chunk, q_ref, k_ref, v_ref, u_ref, w_ref, stat_ref):
    step = pl.program_id(0)
    group, _, count = q_ref.shape
    half = count // 2

    def attend(item, keys, start, side, inner, limit):
        head = step * group + item
        cols = pl.ds(start, chunk)
        scores = dot(keys, q_ref[item, :, cols])
        top = jnp.max(scores, 0, keepdims=True) if limit is None else limit
        weights = jnp.exp(scores - top)
        weighted = dot(v_ref[item], weights.astype(BF16))
        w_ref[side, item, :, pl.ds(inner, chunk)] = weighted
        stat_ref[0, pl.ds(head, 1), cols] = top
        stat_ref[1, pl.ds(head, 1), cols] = jnp.sum(weights, 0, keepdims=True)
        stat_ref[2, pl.ds(head, 1), cols] = jnp.sum(
            u_ref[item, :, cols].astype(F32) * weighted, 0, keepdims=True
        )

    limits = []
    for item in range(group):
        q, k = q_ref[item].astype(F32), k_ref[item].astype(F32)
        longest = jnp.max(jnp.sum(k * k, 0, keepdims=True), 1, keepdims=True)
        limits.append(jnp.sqrt(jnp.sum(q * q, 0, keepdims=True) * longest) * 1.0001)
    highest = functools.reduce(jnp.maximum, [jnp.max(limit) for limit in limits])

    @pl.when(highest < 32.0)
    def _():
        for item in range(group):
            keys = k_ref[item].astype(F32).T.astype(BF16)
            for start in range(0, count, chunk):
                limit = limits[item][:, start : start + chunk]
                attend(item, keys, start, start // half, start % half, limit)

    @pl.when(jnp.logical_not(highest < 32.0))
    def _():
        per_side = half // chunk

        @pl.loop(0, group * 2 * per_side)
        def _(turn):
            item, side, place = turn // (2 * per_side), turn // per_side % 2, turn % per_side
            inner = pl.multiple_of(place * chunk, chunk)
            start = pl.multiple_of(side * half + inner, chunk)
            keys = k_ref[item].astype(F32).T.astype(BF16)
            attend(item, keys, start, side, inner, None)


def forward(q, k, v, u):
    heads, _, count = q.shape
    tokens = k.shape[2]
    group = 2
    per_head = lambda n: pl.BlockSpec((group, HD, n), lambda h: (h, 0, 0))
    return pl.pallas_call(
        functools.partial(forward_kernel, min(256, count // 2)),
        grid=(heads // group,),
        in_specs=[per_head(count), per_head(tokens), per_head(tokens), per_head(count)],
        out_specs=[
            pl.BlockSpec((2, group, HD, count // 2), lambda h: (0, h, 0, 0)),
            pl.BlockSpec((3, heads, count), lambda h: (0, 0, 0)),
        ],
        out_shape=[
            jax.ShapeDtypeStruct((2, heads, HD, count // 2), F32),
            jax.ShapeDtypeStruct((3, heads, count), F32),
        ],
        compiler_params=params(),
        cost_estimate=cost(16 * heads * count * tokens * HD, 9e6),
        name="attend",
    )(q, k, v, u)


def backward_kernel(
    chunk, q_ref, k_ref, v_ref, u_ref, stat_ref, dq_ref, dkv_ref, done_ref
):
    group, _, count = q_ref.shape
    half = count // 2
    for item in range(group):
        head = pl.program_id(0) * group + item
        keys_t = k_ref[item]
        keys = keys_t.astype(F32).T.astype(BF16)
        vals = v_ref[item].astype(F32).T.astype(BF16)
        key_grad = jnp.zeros(keys.shape, F32)
        value_grad = jnp.zeros(vals.shape, F32)
        total = stat_ref[1, pl.ds(head, 1), :]
        lse = stat_ref[0, pl.ds(head, 1), :] + jnp.log(total)
        delta = stat_ref[2, pl.ds(head, 1), :] / total
        for start in range(0, count, chunk):
            cols = slice(start, start + chunk)
            q = q_ref[item, :, cols]
            u = u_ref[item, :, cols]
            probs = jnp.exp(dot(keys, q) - lse[:, cols])
            grad = (probs * (dot(vals, u) - delta[:, cols])).astype(BF16)
            value_grad += dot(probs.astype(BF16), u.astype(F32).T.astype(BF16))
            key_grad += dot(grad, q.astype(F32).T.astype(BF16))
            side, inner = divmod(start, half)
            dq_ref[side, item, :, inner : inner + chunk] = dot(keys_t, grad)
        dkv_ref[0, item] = key_grad.T.astype(BF16)
        dkv_ref[1, item] = value_grad.T.astype(BF16)
    done_ref[...] = jnp.zeros_like(done_ref)


def backward(q, k, v, u, stats):
    heads, _, count = q.shape
    tokens = k.shape[2]
    group = 1
    per_head = lambda n: pl.BlockSpec((group, HD, n), lambda h: (h, 0, 0))
    return pl.pallas_call(
        functools.partial(backward_kernel, min(256, count // 2)),
        grid=(heads // group,),
        in_specs=[
            per_head(count), per_head(tokens), per_head(tokens), per_head(count),
            pl.BlockSpec((3, heads, count), lambda h: (0, 0, 0)),
        ],
        out_specs=[
            pl.BlockSpec((2, group, HD, count // 2), lambda h: (0, h, 0, 0)),
            pl.BlockSpec((2, group, HD, tokens), lambda h: (0, h, 0, 0)),
            pl.BlockSpec((8, 128), lambda h: (0, 0)),
        ],
        out_shape=[
            jax.ShapeDtypeStruct((2, heads, HD, count // 2), F32),
            jax.ShapeDtypeStruct((2, heads, HD, tokens), BF16),
            jax.ShapeDtypeStruct((8, 128), F32),
        ],
        compiler_params=params(),
        cost_estimate=cost(40 * heads * count * tokens * HD, 9e6),
        name="attend_back",
    )(q, k, v, u, stats)


def sum_kernel(pieces_ref, *refs):
    refs[-1][...] = jnp.sum(pieces_ref[...], 0)


def sum_pieces(pieces, *after):
    return pl.pallas_call(
        sum_kernel,
        in_specs=[pl.BlockSpec(memory_space=pltpu.VMEM)] + [pl.BlockSpec(memory_space=pl.ANY)] * len(after),
        out_shape=jax.ShapeDtypeStruct(pieces.shape[1:], F32),
        compiler_params=params(),
        cost_estimate=cost(pieces.size, 4 * pieces.size),
        name="sum_pieces",
    )(pieces, *after)


def out_kernel(att_ref, rows_ref, own_ref, other_ref, after_ref, grad_ref, keep_ref, send_ref):
    att = att_ref[0].reshape(own_ref.shape[1], att_ref.shape[3]).astype(BF16)
    term = dot(rows_ref[...], att, NT)

    @pl.when(pl.program_id(0) == 0)
    def _():
        grad_ref[...] = term

    @pl.when(pl.program_id(0) > 0)
    def _():
        grad_ref[...] += term

    send_ref[...] = dot(other_ref[...], att)
    keep_ref[...] = dot(own_ref[...], att)


def out_step(att, rows, own, other, after):
    _, heads, _, half = att.shape
    width, inner = own.shape
    share = rows.shape[0]
    whole = lambda a: pl.BlockSpec(a.shape, lambda i: (0, 0))
    return pl.pallas_call(
        out_kernel,
        grid=(2,),
        in_specs=[
            pl.BlockSpec((1, heads, HD, half), lambda i: (i, 0, 0, 0)),
            pl.BlockSpec((share, half), lambda i: (0, i)),
            whole(own),
            whole(other),
            pl.BlockSpec(memory_space=pl.ANY),
        ],
        out_specs=[
            pl.BlockSpec((share, inner), lambda i: (0, 0)),
            pl.BlockSpec((width, half), lambda i: (0, i)),
            pl.BlockSpec((width, half), lambda i: (0, i)),
        ],
        out_shape=[
            jax.ShapeDtypeStruct((share, inner), F32),
            jax.ShapeDtypeStruct((width, 2 * half), F32),
            jax.ShapeDtypeStruct((width, 2 * half), F32),
        ],
        compiler_params=params(),
        cost_estimate=cost(8 * half * inner * width, 12e6),
        name="project_out",
    )(att, rows, own, other, after)


def query_kernel(pieces_ref, norm_ref, out_ref):
    places, share, _ = out_ref.shape
    heads = places // 2
    total = jnp.sum(pieces_ref[...], 0)
    depth, half = total.shape
    rows = half // heads
    proj = (total * HD ** (-0.5)).astype(BF16)
    term = dot(norm_ref[...], proj, NT)
    for place in range(places):
        strip = place % heads * rows
        out_ref[place, :, :depth] = term[place * share : (place + 1) * share, :]
        out_ref[place, :depth, 128 : 128 + rows] = total[:, strip : strip + rows]


def query_step(pieces, norm, places):
    _, depth, half = pieces.shape
    width = norm.shape[0]
    return pl.pallas_call(
        query_kernel,
        out_shape=jax.ShapeDtypeStruct((places, width // places, 256), F32),
        compiler_params=params(),
        cost_estimate=cost(2 * half * width * depth, 6e6),
        name="query_grad",
    )(pieces, norm)


def latent_kernel(pieces_ref, qw_ref, latents_ref, cot_ref, out_ref):
    heads, depth, rows = pieces_ref.shape
    proj = pieces_ref[...].reshape(heads * depth, rows) * HD ** (-0.5)
    up = dot(proj.T.astype(BF16), qw_ref[...])
    hat, inv = layer_norm(latents_ref[...].astype(F32))
    term = norm_backward(hat, inv, up) + cot_ref[...].astype(F32) / 2
    size = out_ref.shape[2]
    for block in range(out_ref.shape[0]):
        out_ref[block] = term[:, block * size : (block + 1) * size]


def latent_step(pieces, qw, latents, cot, blocks):
    rows, width = latents.shape
    return pl.pallas_call(
        latent_kernel,
        out_shape=jax.ShapeDtypeStruct((blocks, rows, width // blocks), F32),
        compiler_params=params(),
        cost_estimate=cost(2 * rows * qw.size, 4e6),
        name="latent_grad",
    )(pieces, qw, latents, cot)


def shift(value, axis, by, side=None, minor=True):
    size = lax.axis_size(axis)
    if side is None:
        pairs = [(i, (i + by) % size) for i in range(size)]
    elif minor:
        pairs = [(i, i // side * side + (i % side + by) % side) for i in range(size)]
    else:
        pairs = [(i, (i + by * side) % size) for i in range(size)]
    return lax.ppermute(value, axis, pairs)


def pick(blocks, index):
    return lax.dynamic_index_in_dim(blocks, index, 0, False)


def scatter_sum(blocks, axis, place, side=None, minor=True):
    size = blocks.shape[0]
    total = pick(blocks, place)
    for by in range(1, size):
        total = total + shift(pick(blocks, (place + by) % size), axis, by, side, minor)
    return total


def relay_start(blocks, place, cut, send):
    far = pick(blocks, (place + 2) % 4)
    return send(far[:cut], 1), send(far[cut:], -1)


def relay_end(blocks, place, cut, send, front, back):
    ahead = pick(blocks, (place + 1) % 4)
    behind = pick(blocks, (place + 3) % 4)
    ahead = jnp.concatenate([ahead[:cut] + front, ahead[cut:]], 0)
    behind = jnp.concatenate([behind[:cut], behind[cut:] + back], 0)
    return pick(blocks, place) + send(ahead, 1) + send(behind, -1)


def merge_stats(stats, side, minor):
    parts = [stats] + [shift(stats, "seq", by, side, minor) for by in range(1, side)]
    top = functools.reduce(jnp.maximum, [p[0] for p in parts])
    factors = [jnp.exp(p[0] - top) for p in parts]
    total = sum(p[1] * f for p, f in zip(parts, factors))
    delta = sum(p[2] * f for p, f in zip(parts, factors))
    return jnp.stack([top, total, delta])


def local(media_tokens, latents, query_weight, key_weight, value_weight, out_weight, cotangent):
    inner = query_weight.shape[1]
    width = query_weight.shape[0]
    heads = inner // HD
    count = latents.shape[0]
    half = count // 2
    seq, tp, dp = (lax.axis_index(a) for a in ("seq", "tp", "dp"))
    seqs, tps, dps = (lax.axis_size(a) for a in ("seq", "tp", "dp"))
    side = 4
    share = width // seqs
    part = share // dps
    padded = -(-part // 8) * 8
    rows = count // seqs
    upstream = cotangent[0]
    query_turned = query_weight.T

    media_norm, latent_norm, k, v, q, u = project(
        media_tokens[0], latents, upstream, query_turned, key_weight.T, value_weight.T, out_weight
    )
    weighted, stats = forward(q, k, v, u)

    whole = merge_stats(merge_stats(stats, side, True), side, False)
    factor = (jnp.exp(stats[0] - whole[0]) / whole[1]).reshape(heads, 2, 1, half).transpose(1, 0, 2, 3)

    scaled = (weighted * factor).reshape(seqs, HD, half)
    attended_pieces = lax.all_to_all(scaled, "seq", 0, 0, tiled=True)
    dq, dkv, done = backward(q, k, v, u, whole)
    seq, tp, done = lax.optimization_barrier((seq, tp, done))

    query_pieces = lax.all_to_all(dq.reshape(seqs, HD, half), "seq", 0, 0, tiled=True)

    major, minor = seq // side, seq % side
    blocks = media_norm.reshape(seqs, dps, part, -1).transpose(1, 0, 2, 3)
    blocks = jnp.pad(blocks, ((0, 0), (0, 0), (0, padded - part), (0, 0)))
    blocks = blocks.reshape(dps * seqs * padded, -1)
    grads = dkv.reshape(2 * inner, -1)
    split = (inner // 128 + 1) * 128
    terms = [dot(blocks, grads[:split], NT), dot(blocks, grads[split:], NT)]
    terms = [t.reshape(dps, seqs * padded, -1) for t in terms]
    ring = (dp, seqs * padded // 2, lambda value, by: shift(value, "dp", by))
    halves = [relay_start(t, *ring) for t in terms]
    attended = sum_pieces(attended_pieces, terms[1], *halves[0])
    terms = [relay_end(t, *ring, *h) for t, h in zip(terms, halves)]
    first, second = (t.reshape(side, side, padded, -1) for t in terms)
    first = scatter_sum(first.transpose(1, 0, 2, 3), "seq", minor, side, True)
    first = scatter_sum(first, "seq", major, side, False)
    second = scatter_sum(second, "seq", major, side, False)
    second = scatter_sum(second, "seq", minor, side, True)
    grad_key = first[:part, :inner]
    grad_value = jnp.concatenate([first[:part, inner:], second[:part]], 1)

    side_of = seq // heads
    norm_half = lax.dynamic_slice_in_dim(latent_norm, side_of * half, half, 1)
    term = query_step(query_pieces, norm_half, seqs)
    sent = lax.all_to_all(term, "seq", 0, 0, tiled=True)
    strips = lax.dynamic_slice(sent, (side_of * heads, 0, 128), (heads, HD, rows))
    latent_rows = lax.dynamic_slice_in_dim(latents, seq * rows, rows, 0)
    cot_rows = lax.dynamic_slice_in_dim(upstream, seq * rows, rows, 0)
    back = latent_step(strips, query_turned, latent_rows, cot_rows, tps * dps)
    blocks = (sent[:heads, :, :HD] + sent[heads:, :, :HD]).transpose(1, 0, 2)
    grad_query = scatter_sum(blocks.reshape(dps, part, inner), "dp", dp)
    grad_latents = jnp.sum(lax.all_to_all(back, ("tp", "dp"), 0, 0, tiled=True), 0)

    attended = lax.all_gather(attended, "seq")
    cot_cols = lax.dynamic_slice_in_dim(upstream, seq * share, share, 1).T
    own = lax.dynamic_slice_in_dim(out_weight, tp * inner, inner, 1).T
    other = lax.dynamic_slice_in_dim(out_weight, (1 - tp) * inner, inner, 1).T
    latent_cols = lax.dynamic_slice_in_dim(latents, tp * inner, inner, 1).T
    out_rows, keep, away = out_step(
        attended.reshape(2, heads, HD, half), cot_cols, own, other, sent
    )
    arrived = lax.ppermute(away, "tp", [(0, 1), (1, 0)])
    resampled = (latent_cols.astype(F32) + (keep + arrived)).astype(BF16).T[None]
    grad_out = scatter_sum(out_rows.reshape(dps, part, inner), "dp", dp).T

    return (resampled, grad_latents, grad_query, grad_key, grad_value, grad_out)


def solution(mesh):
    placed = (
        P("dp", "seq", None),
        P(),
        P(None, "tp"),
        P(None, "tp"),
        P(None, "tp"),
        P("tp", None),
        P("dp", None, None),
    )
    return jax.shard_map(
        local,
        mesh=mesh,
        in_specs=placed,
        out_specs=(
            P("dp", None, "tp"),
            P("seq", ("tp", "dp")),
            P(("seq", "dp"), "tp"),
            P(("seq", "dp"), "tp"),
            P(("seq", "dp"), "tp"),
            P("tp", ("seq", "dp")),
        ),
        check_vma=False,
    )
```

```python
import functools

import jax
import jax.numpy as jnp
from jax import lax
from jax.experimental import pallas as pl
from jax.experimental.pallas import tpu as pltpu
from jax.sharding import PartitionSpec as P

HD = 88
VMEM = 56 * 1024 * 1024
F32 = jnp.float32
BF16 = jnp.bfloat16
NT = (((1,), (1,)), ((), ()))
TN = (((0,), (0,)), ((), ()))


def params():
    return pltpu.CompilerParams(vmem_limit_bytes=VMEM)


def cost(flops, size):
    return pl.CostEstimate(flops=int(flops), bytes_accessed=int(size), transcendentals=0)


def dot(a, b, dims=(((1,), (0,)), ((), ()))):
    return lax.dot_general(a, b, dims, preferred_element_type=F32)


def layer_norm(rows):
    average = jnp.mean(rows, -1, keepdims=True)
    centered = rows - average
    variance = jnp.mean(centered * centered, -1, keepdims=True)
    inv_std = lax.rsqrt(variance + 1e-05)
    return (centered * inv_std, inv_std)


def norm_backward(normed, inv_std, upstream):
    mean_up = jnp.mean(upstream, -1, keepdims=True)
    mean_cross = jnp.mean(upstream * normed, -1, keepdims=True)
    return inv_std * (upstream - mean_up - normed * mean_cross)


def project_kernel(media, kw, vw, latents, qw, cot, ow, mn, ln, k, v, q, u, *scratch):
    arrays = [media, kw, vw, latents, qw, cot, ow, mn, ln, k, v, q, u]
    held, (arrive, leave) = scratch[: len(arrays)], scratch[len(arrays) :]
    media_at, kw_at, vw_at, latents_at, qw_at, cot_at, ow_at, mn_at, ln_at, k_at, v_at, q_at, u_at = held
    fetch = [pltpu.make_async_copy(arrays[i], held[i], arrive.at[i]) for i in range(7)]
    store = [pltpu.make_async_copy(held[7 + i], arrays[7 + i], leave.at[i]) for i in range(6)]
    for copy in fetch:
        copy.start()

    def chunks(count, body):
        size = min(256, count)

        @pl.loop(0, count // size)
        def _(i):
            body(pl.ds(pl.multiple_of(i * size, size), size))

    def normalise(source, target):
        def body(rows):
            target[:, rows] = layer_norm(source[rows, :].astype(F32))[0].T.astype(BF16)

        chunks(source.shape[0], body)

    def split(target, cols, value):
        for head in range(target.shape[0]):
            target[head, :, cols] = value[head * HD : (head + 1) * HD, :].astype(BF16)

    fetch[0].wait()
    normalise(media_at, mn_at)
    store[0].start()
    for i, weight, target in ((1, kw_at, k_at), (2, vw_at, v_at)):
        fetch[i].wait()
        chunks(
            mn_at.shape[1],
            lambda cols: split(target, cols, dot(weight[...], mn_at[:, cols])),
        )
        store[1 + i].start()
    fetch[3].wait()
    normalise(latents_at, ln_at)
    store[1].start()
    fetch[4].wait()
    chunks(
        ln_at.shape[1],
        lambda cols: split(q_at, cols, dot(qw_at[...], ln_at[:, cols]) * HD ** (-0.5)),
    )
    store[4].start()
    fetch[5].wait()
    fetch[6].wait()
    chunks(
        cot_at.shape[0],
        lambda rows: split(u_at, rows, dot(ow_at[...], cot_at[rows, :], NT)),
    )
    store[5].start()
    for copy in store:
        copy.wait()


def project(media, latents, cot, qw, kw, vw, ow):
    tokens, width = media.shape
    count = latents.shape[0]
    inner = qw.shape[0]
    heads = inner // HD
    ins = (media, kw, vw, latents, qw, cot, ow)
    outs = [
        jax.ShapeDtypeStruct(size, BF16)
        for size in (
            (width, tokens), (width, count),
            (heads, HD, tokens), (heads, HD, tokens), (heads, HD, count), (heads, HD, count),
        )
    ]
    anywhere = pl.BlockSpec(memory_space=pl.ANY)
    return pl.pallas_call(
        project_kernel,
        in_specs=[anywhere] * len(ins),
        out_specs=[anywhere] * len(outs),
        out_shape=outs,
        scratch_shapes=[pltpu.VMEM(a.shape, BF16) for a in (*ins, *outs)]
        + [pltpu.SemaphoreType.DMA((len(ins),)), pltpu.SemaphoreType.DMA((len(outs),))],
        compiler_params=params(),
        cost_estimate=cost(4 * (tokens + count) * width * inner, 24e6),
        name="project",
    )(*ins)


def forward_kernel(chunk, q_ref, k_ref, v_ref, u_ref, w_ref, stat_ref):
    step = pl.program_id(0)
    group, _, count = q_ref.shape
    half = count // 2

    def attend(item, keys, start, side, inner, limit):
        head = step * group + item
        cols = pl.ds(start, chunk)
        scores = dot(keys, q_ref[item, :, cols])
        top = jnp.max(scores, 0, keepdims=True) if limit is None else limit
        weights = jnp.exp(scores - top)
        weighted = dot(v_ref[item], weights.astype(BF16))
        w_ref[side, item, :, pl.ds(inner, chunk)] = weighted
        stat_ref[0, pl.ds(head, 1), cols] = top
        stat_ref[1, pl.ds(head, 1), cols] = jnp.sum(weights, 0, keepdims=True)
        stat_ref[2, pl.ds(head, 1), cols] = jnp.sum(
            u_ref[item, :, cols].astype(F32) * weighted, 0, keepdims=True
        )

    limits = []
    for item in range(group):
        q, k = q_ref[item].astype(F32), k_ref[item].astype(F32)
        longest = jnp.max(jnp.sum(k * k, 0, keepdims=True), 1, keepdims=True)
        limits.append(jnp.sqrt(jnp.sum(q * q, 0, keepdims=True) * longest) * 1.0001)
    highest = functools.reduce(jnp.maximum, [jnp.max(limit) for limit in limits])

    @pl.when(highest < 32.0)
    def _():
        for item in range(group):
            keys = k_ref[item].astype(F32).T.astype(BF16)
            for start in range(0, count, chunk):
                limit = limits[item][:, start : start + chunk]
                attend(item, keys, start, start // half, start % half, limit)

    @pl.when(jnp.logical_not(highest < 32.0))
    def _():
        per_side = half // chunk

        @pl.loop(0, group * 2 * per_side)
        def _(turn):
            item, side, place = turn // (2 * per_side), turn // per_side % 2, turn % per_side
            inner = pl.multiple_of(place * chunk, chunk)
            start = pl.multiple_of(side * half + inner, chunk)
            keys = k_ref[item].astype(F32).T.astype(BF16)
            attend(item, keys, start, side, inner, None)


def forward(q, k, v, u):
    heads, _, count = q.shape
    tokens = k.shape[2]
    group = 2
    per_head = lambda n: pl.BlockSpec((group, HD, n), lambda h: (h, 0, 0))
    return pl.pallas_call(
        functools.partial(forward_kernel, min(256, count // 2)),
        grid=(heads // group,),
        in_specs=[per_head(count), per_head(tokens), per_head(tokens), per_head(count)],
        out_specs=[
            pl.BlockSpec((2, group, HD, count // 2), lambda h: (0, h, 0, 0)),
            pl.BlockSpec((3, heads, count), lambda h: (0, 0, 0)),
        ],
        out_shape=[
            jax.ShapeDtypeStruct((2, heads, HD, count // 2), F32),
            jax.ShapeDtypeStruct((3, heads, count), F32),
        ],
        compiler_params=params(),
        cost_estimate=cost(16 * heads * count * tokens * HD, 9e6),
        name="attend",
    )(q, k, v, u)


def backward_kernel(
    chunk, q_ref, k_ref, v_ref, u_ref, stat_ref, dq_ref, dkv_ref, done_ref
):
    group, _, count = q_ref.shape
    half = count // 2
    for item in range(group):
        head = pl.program_id(0) * group + item
        keys_t = k_ref[item]
        keys = keys_t.astype(F32).T.astype(BF16)
        vals = v_ref[item].astype(F32).T.astype(BF16)
        key_grad = jnp.zeros(keys.shape, F32)
        value_grad = jnp.zeros(vals.shape, F32)
        total = stat_ref[1, pl.ds(head, 1), :]
        lse = stat_ref[0, pl.ds(head, 1), :] + jnp.log(total)
        delta = stat_ref[2, pl.ds(head, 1), :] / total
        for start in range(0, count, chunk):
            cols = slice(start, start + chunk)
            q = q_ref[item, :, cols]
            u = u_ref[item, :, cols]
            probs = jnp.exp(dot(keys, q) - lse[:, cols])
            grad = (probs * (dot(vals, u) - delta[:, cols])).astype(BF16)
            value_grad += dot(probs.astype(BF16), u.astype(F32).T.astype(BF16))
            key_grad += dot(grad, q.astype(F32).T.astype(BF16))
            side, inner = divmod(start, half)
            dq_ref[side, item, :, inner : inner + chunk] = dot(keys_t, grad)
        dkv_ref[0, item] = key_grad.T.astype(BF16)
        dkv_ref[1, item] = value_grad.T.astype(BF16)
    done_ref[...] = jnp.zeros_like(done_ref)


def backward(q, k, v, u, stats):
    heads, _, count = q.shape
    tokens = k.shape[2]
    group = 1
    per_head = lambda n: pl.BlockSpec((group, HD, n), lambda h: (h, 0, 0))
    return pl.pallas_call(
        functools.partial(backward_kernel, min(256, count // 2)),
        grid=(heads // group,),
        in_specs=[
            per_head(count), per_head(tokens), per_head(tokens), per_head(count),
            pl.BlockSpec((3, heads, count), lambda h: (0, 0, 0)),
        ],
        out_specs=[
            pl.BlockSpec((2, group, HD, count // 2), lambda h: (0, h, 0, 0)),
            pl.BlockSpec((2, group, HD, tokens), lambda h: (0, h, 0, 0)),
            pl.BlockSpec((8, 128), lambda h: (0, 0)),
        ],
        out_shape=[
            jax.ShapeDtypeStruct((2, heads, HD, count // 2), F32),
            jax.ShapeDtypeStruct((2, heads, HD, tokens), BF16),
            jax.ShapeDtypeStruct((8, 128), F32),
        ],
        compiler_params=params(),
        cost_estimate=cost(40 * heads * count * tokens * HD, 9e6),
        name="attend_back",
    )(q, k, v, u, stats)


def sum_kernel(pieces_ref, *refs):
    refs[-1][...] = jnp.sum(pieces_ref[...], 0)


def sum_pieces(pieces, *after):
    return pl.pallas_call(
        sum_kernel,
        in_specs=[pl.BlockSpec(memory_space=pltpu.VMEM)] + [pl.BlockSpec(memory_space=pl.ANY)] * len(after),
        out_shape=jax.ShapeDtypeStruct(pieces.shape[1:], F32),
        compiler_params=params(),
        cost_estimate=cost(pieces.size, 4 * pieces.size),
        name="sum_pieces",
    )(pieces, *after)


def out_kernel(att_ref, rows_ref, own_ref, other_ref, after_ref, grad_ref, keep_ref, send_ref):
    att = att_ref[0].reshape(own_ref.shape[1], att_ref.shape[3]).astype(BF16)
    term = dot(rows_ref[...], att, NT)

    @pl.when(pl.program_id(0) == 0)
    def _():
        grad_ref[...] = term

    @pl.when(pl.program_id(0) > 0)
    def _():
        grad_ref[...] += term

    send_ref[...] = dot(other_ref[...], att)
    keep_ref[...] = dot(own_ref[...], att)


def out_step(att, rows, own, other, after):
    _, heads, _, half = att.shape
    width, inner = own.shape
    share = rows.shape[0]
    whole = lambda a: pl.BlockSpec(a.shape, lambda i: (0, 0))
    return pl.pallas_call(
        out_kernel,
        grid=(2,),
        in_specs=[
            pl.BlockSpec((1, heads, HD, half), lambda i: (i, 0, 0, 0)),
            pl.BlockSpec((share, half), lambda i: (0, i)),
            whole(own),
            whole(other),
            pl.BlockSpec(memory_space=pl.ANY),
        ],
        out_specs=[
            pl.BlockSpec((share, inner), lambda i: (0, 0)),
            pl.BlockSpec((width, half), lambda i: (0, i)),
            pl.BlockSpec((width, half), lambda i: (0, i)),
        ],
        out_shape=[
            jax.ShapeDtypeStruct((share, inner), F32),
            jax.ShapeDtypeStruct((width, 2 * half), F32),
            jax.ShapeDtypeStruct((width, 2 * half), F32),
        ],
        compiler_params=params(),
        cost_estimate=cost(8 * half * inner * width, 12e6),
        name="project_out",
    )(att, rows, own, other, after)


def query_kernel(pieces_ref, norm_ref, out_ref):
    places, share, _ = out_ref.shape
    heads = places // 2
    total = jnp.sum(pieces_ref[...], 0)
    depth, half = total.shape
    rows = half // heads
    proj = (total * HD ** (-0.5)).astype(BF16)
    term = dot(norm_ref[...], proj, NT)
    for place in range(places):
        strip = place % heads * rows
        out_ref[place, :, :depth] = term[place * share : (place + 1) * share, :]
        out_ref[place, :depth, 128 : 128 + rows] = total[:, strip : strip + rows]


def query_step(pieces, norm, places):
    _, depth, half = pieces.shape
    width = norm.shape[0]
    return pl.pallas_call(
        query_kernel,
        out_shape=jax.ShapeDtypeStruct((places, width // places, 256), F32),
        compiler_params=params(),
        cost_estimate=cost(2 * half * width * depth, 6e6),
        name="query_grad",
    )(pieces, norm)


def latent_kernel(pieces_ref, qw_ref, latents_ref, cot_ref, out_ref):
    heads, depth, rows = pieces_ref.shape
    proj = pieces_ref[...].reshape(heads * depth, rows) * HD ** (-0.5)
    up = dot(proj.T.astype(BF16), qw_ref[...])
    hat, inv = layer_norm(latents_ref[...].astype(F32))
    term = norm_backward(hat, inv, up) + cot_ref[...].astype(F32) / 2
    size = out_ref.shape[2]
    for block in range(out_ref.shape[0]):
        out_ref[block] = term[:, block * size : (block + 1) * size]


def latent_step(pieces, qw, latents, cot, blocks):
    rows, width = latents.shape
    return pl.pallas_call(
        latent_kernel,
        out_shape=jax.ShapeDtypeStruct((blocks, rows, width // blocks), F32),
        compiler_params=params(),
        cost_estimate=cost(2 * rows * qw.size, 4e6),
        name="latent_grad",
    )(pieces, qw, latents, cot)


def shift(value, axis, by, side=None, minor=True):
    size = lax.axis_size(axis)
    if side is None:
        pairs = [(i, (i + by) % size) for i in range(size)]
    elif minor:
        pairs = [(i, i // side * side + (i % side + by) % side) for i in range(size)]
    else:
        pairs = [(i, (i + by * side) % size) for i in range(size)]
    return lax.ppermute(value, axis, pairs)


def pick(blocks, index):
    return lax.dynamic_index_in_dim(blocks, index, 0, False)


def scatter_sum(blocks, axis, place, side=None, minor=True):
    size = blocks.shape[0]
    total = pick(blocks, place)
    for by in range(1, size):
        total = total + shift(pick(blocks, (place + by) % size), axis, by, side, minor)
    return total


def relay_start(blocks, place, cut, send):
    far = pick(blocks, (place + 2) % 4)
    return send(far[:cut], 1), send(far[cut:], -1)


def relay_end(blocks, place, cut, send, front, back):
    ahead = pick(blocks, (place + 1) % 4)
    behind = pick(blocks, (place + 3) % 4)
    ahead = jnp.concatenate([ahead[:cut] + front, ahead[cut:]], 0)
    behind = jnp.concatenate([behind[:cut], behind[cut:] + back], 0)
    return pick(blocks, place) + send(ahead, 1) + send(behind, -1)


def merge_stats(stats, side, minor):
    parts = [stats] + [shift(stats, "seq", by, side, minor) for by in range(1, side)]
    top = functools.reduce(jnp.maximum, [p[0] for p in parts])
    factors = [jnp.exp(p[0] - top) for p in parts]
    total = sum(p[1] * f for p, f in zip(parts, factors))
    delta = sum(p[2] * f for p, f in zip(parts, factors))
    return jnp.stack([top, total, delta])


def local(media_tokens, latents, query_weight, key_weight, value_weight, out_weight, cotangent):
    inner = query_weight.shape[1]
    width = query_weight.shape[0]
    heads = inner // HD
    count = latents.shape[0]
    half = count // 2
    seq, tp, dp = (lax.axis_index(a) for a in ("seq", "tp", "dp"))
    seqs, tps, dps = (lax.axis_size(a) for a in ("seq", "tp", "dp"))
    side = 4
    share = width // seqs
    part = share // dps
    padded = -(-part // 8) * 8
    rows = count // seqs
    upstream = cotangent[0]
    query_turned = query_weight.T

    media_norm, latent_norm, k, v, q, u = project(
        media_tokens[0], latents, upstream, query_turned, key_weight.T, value_weight.T, out_weight
    )
    weighted, stats = forward(q, k, v, u)

    whole = merge_stats(merge_stats(stats, side, True), side, False)
    factor = (jnp.exp(stats[0] - whole[0]) / whole[1]).reshape(heads, 2, 1, half).transpose(1, 0, 2, 3)

    scaled = (weighted * factor).reshape(seqs, HD, half)
    attended_pieces = lax.all_to_all(scaled, "seq", 0, 0, tiled=True)
    dq, dkv, done = backward(q, k, v, u, whole)
    seq, tp, done = lax.optimization_barrier((seq, tp, done))

    query_pieces = lax.all_to_all(dq.reshape(seqs, HD, half), "seq", 0, 0, tiled=True)

    major, minor = seq // side, seq % side
    blocks = media_norm.reshape(seqs, dps, part, -1).transpose(1, 0, 2, 3)
    blocks = jnp.pad(blocks, ((0, 0), (0, 0), (0, padded - part), (0, 0)))
    blocks = blocks.reshape(dps * seqs * padded, -1)
    grads = dkv.reshape(2 * inner, -1)
    split = (inner // 128 + 1) * 128
    terms = [dot(blocks, grads[:split], NT), dot(blocks, grads[split:], NT)]
    terms = [t.reshape(dps, seqs * padded, -1) for t in terms]
    ring = (dp, seqs * padded // 2, lambda value, by: shift(value, "dp", by))
    halves = [relay_start(t, *ring) for t in terms]
    attended = sum_pieces(attended_pieces, terms[1], *halves[0])
    terms = [relay_end(t, *ring, *h) for t, h in zip(terms, halves)]
    first, second = (t.reshape(side, side, padded, -1) for t in terms)
    first = scatter_sum(first.transpose(1, 0, 2, 3), "seq", minor, side, True)
    first = scatter_sum(first, "seq", major, side, False)
    second = scatter_sum(second, "seq", major, side, False)
    second = scatter_sum(second, "seq", minor, side, True)
    grad_key = first[:part, :inner]
    grad_value = jnp.concatenate([first[:part, inner:], second[:part]], 1)

    side_of = seq // heads
    norm_half = lax.dynamic_slice_in_dim(latent_norm, side_of * half, half, 1)
    term = query_step(query_pieces, norm_half, seqs)
    sent = lax.all_to_all(term, "seq", 0, 0, tiled=True)
    strips = lax.dynamic_slice(sent, (side_of * heads, 0, 128), (heads, HD, rows))
    latent_rows = lax.dynamic_slice_in_dim(latents, seq * rows, rows, 0)
    cot_rows = lax.dynamic_slice_in_dim(upstream, seq * rows, rows, 0)
    back = latent_step(strips, query_turned, latent_rows, cot_rows, tps * dps)
    blocks = (sent[:heads, :, :HD] + sent[heads:, :, :HD]).transpose(1, 0, 2)
    grad_query = scatter_sum(blocks.reshape(dps, part, inner), "dp", dp)
    grad_latents = jnp.sum(lax.all_to_all(back, ("tp", "dp"), 0, 0, tiled=True), 0)

    attended = lax.all_gather(attended, "seq")
    cot_cols = lax.dynamic_slice_in_dim(upstream, seq * share, share, 1).T
    own = lax.dynamic_slice_in_dim(out_weight, tp * inner, inner, 1).T
    other = lax.dynamic_slice_in_dim(out_weight, (1 - tp) * inner, inner, 1).T
    latent_cols = lax.dynamic_slice_in_dim(latents, tp * inner, inner, 1).T
    out_rows, keep, away = out_step(
        attended.reshape(2, heads, HD, half), cot_cols, own, other, back
    )
    arrived = lax.ppermute(away, "tp", [(0, 1), (1, 0)])
    resampled = (latent_cols.astype(F32) + (keep + arrived)).astype(BF16).T[None]
    grad_out = scatter_sum(out_rows.reshape(dps, part, inner), "dp", dp).T

    return (resampled, grad_latents, grad_query, grad_key, grad_value, grad_out)


def solution(mesh):
    placed = (
        P("dp", "seq", None),
        P(),
        P(None, "tp"),
        P(None, "tp"),
        P(None, "tp"),
        P("tp", None),
        P("dp", None, None),
    )
    return jax.shard_map(
        local,
        mesh=mesh,
        in_specs=placed,
        out_specs=(
            P("dp", None, "tp"),
            P("seq", ("tp", "dp")),
            P(("seq", "dp"), "tp"),
            P(("seq", "dp"), "tp"),
            P(("seq", "dp"), "tp"),
            P("tp", ("seq", "dp")),
        ),
        check_vma=False,
    )
```

```python
import functools

import jax
import jax.numpy as jnp
from jax import lax
from jax.experimental import pallas as pl
from jax.experimental.pallas import tpu as pltpu
from jax.sharding import PartitionSpec as P

HD = 88
VMEM = 56 * 1024 * 1024
F32 = jnp.float32
BF16 = jnp.bfloat16
NT = (((1,), (1,)), ((), ()))
TN = (((0,), (0,)), ((), ()))


def params():
    return pltpu.CompilerParams(vmem_limit_bytes=VMEM)


def cost(flops, size):
    return pl.CostEstimate(flops=int(flops), bytes_accessed=int(size), transcendentals=0)


def dot(a, b, dims=(((1,), (0,)), ((), ()))):
    return lax.dot_general(a, b, dims, preferred_element_type=F32)


def layer_norm(rows):
    average = jnp.mean(rows, -1, keepdims=True)
    centered = rows - average
    variance = jnp.mean(centered * centered, -1, keepdims=True)
    inv_std = lax.rsqrt(variance + 1e-05)
    return (centered * inv_std, inv_std)


def norm_backward(normed, inv_std, upstream):
    mean_up = jnp.mean(upstream, -1, keepdims=True)
    mean_cross = jnp.mean(upstream * normed, -1, keepdims=True)
    return inv_std * (upstream - mean_up - normed * mean_cross)


def project_kernel(media, kw, vw, latents, qw, cot, ow, mn, ln, k, v, q, u, *scratch):
    arrays = [media, kw, vw, latents, qw, cot, ow, mn, ln, k, v, q, u]
    held, (arrive, leave) = scratch[: len(arrays)], scratch[len(arrays) :]
    media_at, kw_at, vw_at, latents_at, qw_at, cot_at, ow_at, mn_at, ln_at, k_at, v_at, q_at, u_at = held
    fetch = [pltpu.make_async_copy(arrays[i], held[i], arrive.at[i]) for i in range(7)]
    store = [pltpu.make_async_copy(held[7 + i], arrays[7 + i], leave.at[i]) for i in range(6)]
    for copy in fetch:
        copy.start()

    def chunks(count, body):
        size = min(256, count)

        @pl.loop(0, count // size)
        def _(i):
            body(pl.ds(pl.multiple_of(i * size, size), size))

    def normalise(source, target):
        def body(rows):
            target[:, rows] = layer_norm(source[rows, :].astype(F32))[0].T.astype(BF16)

        chunks(source.shape[0], body)

    def split(target, cols, value):
        for head in range(target.shape[0]):
            target[head, :, cols] = value[head * HD : (head + 1) * HD, :].astype(BF16)

    fetch[0].wait()
    normalise(media_at, mn_at)
    store[0].start()
    for i, weight, target in ((1, kw_at, k_at), (2, vw_at, v_at)):
        fetch[i].wait()
        chunks(
            mn_at.shape[1],
            lambda cols: split(target, cols, dot(weight[...], mn_at[:, cols])),
        )
        store[1 + i].start()
    fetch[3].wait()
    normalise(latents_at, ln_at)
    store[1].start()
    fetch[4].wait()
    chunks(
        ln_at.shape[1],
        lambda cols: split(q_at, cols, dot(qw_at[...], ln_at[:, cols]) * HD ** (-0.5)),
    )
    store[4].start()
    fetch[5].wait()
    fetch[6].wait()
    chunks(
        cot_at.shape[0],
        lambda rows: split(u_at, rows, dot(ow_at[...], cot_at[rows, :], NT)),
    )
    store[5].start()
    for copy in store:
        copy.wait()


def project(media, latents, cot, qw, kw, vw, ow):
    tokens, width = media.shape
    count = latents.shape[0]
    inner = qw.shape[0]
    heads = inner // HD
    ins = (media, kw, vw, latents, qw, cot, ow)
    outs = [
        jax.ShapeDtypeStruct(size, BF16)
        for size in (
            (width, tokens), (width, count),
            (heads, HD, tokens), (heads, HD, tokens), (heads, HD, count), (heads, HD, count),
        )
    ]
    anywhere = pl.BlockSpec(memory_space=pl.ANY)
    return pl.pallas_call(
        project_kernel,
        in_specs=[anywhere] * len(ins),
        out_specs=[anywhere] * len(outs),
        out_shape=outs,
        scratch_shapes=[pltpu.VMEM(a.shape, BF16) for a in (*ins, *outs)]
        + [pltpu.SemaphoreType.DMA((len(ins),)), pltpu.SemaphoreType.DMA((len(outs),))],
        compiler_params=params(),
        cost_estimate=cost(4 * (tokens + count) * width * inner, 24e6),
        name="project",
    )(*ins)


def forward_kernel(chunk, q_ref, k_ref, v_ref, u_ref, w_ref, stat_ref):
    step = pl.program_id(0)
    group, _, count = q_ref.shape
    half = count // 2

    def attend(item, keys, start, side, inner, limit):
        head = step * group + item
        cols = pl.ds(start, chunk)
        scores = dot(keys, q_ref[item, :, cols])
        top = jnp.max(scores, 0, keepdims=True) if limit is None else limit
        weights = jnp.exp(scores - top)
        weighted = dot(v_ref[item], weights.astype(BF16))
        w_ref[side, item, :, pl.ds(inner, chunk)] = weighted
        stat_ref[0, pl.ds(head, 1), cols] = top
        stat_ref[1, pl.ds(head, 1), cols] = jnp.sum(weights, 0, keepdims=True)
        stat_ref[2, pl.ds(head, 1), cols] = jnp.sum(
            u_ref[item, :, cols].astype(F32) * weighted, 0, keepdims=True
        )

    limits = []
    for item in range(group):
        q, k = q_ref[item].astype(F32), k_ref[item].astype(F32)
        longest = jnp.max(jnp.sum(k * k, 0, keepdims=True), 1, keepdims=True)
        limits.append(jnp.sqrt(jnp.sum(q * q, 0, keepdims=True) * longest) * 1.0001)
    highest = functools.reduce(jnp.maximum, [jnp.max(limit) for limit in limits])

    @pl.when(highest < 32.0)
    def _():
        for item in range(group):
            keys = k_ref[item].astype(F32).T.astype(BF16)
            for start in range(0, count, chunk):
                limit = limits[item][:, start : start + chunk]
                attend(item, keys, start, start // half, start % half, limit)

    @pl.when(jnp.logical_not(highest < 32.0))
    def _():
        per_side = half // chunk

        @pl.loop(0, group * 2 * per_side)
        def _(turn):
            item, side, place = turn // (2 * per_side), turn // per_side % 2, turn % per_side
            inner = pl.multiple_of(place * chunk, chunk)
            start = pl.multiple_of(side * half + inner, chunk)
            keys = k_ref[item].astype(F32).T.astype(BF16)
            attend(item, keys, start, side, inner, None)


def forward(q, k, v, u):
    heads, _, count = q.shape
    tokens = k.shape[2]
    group = 2
    per_head = lambda n: pl.BlockSpec((group, HD, n), lambda h: (h, 0, 0))
    return pl.pallas_call(
        functools.partial(forward_kernel, min(256, count // 2)),
        grid=(heads // group,),
        in_specs=[per_head(count), per_head(tokens), per_head(tokens), per_head(count)],
        out_specs=[
            pl.BlockSpec((2, group, HD, count // 2), lambda h: (0, h, 0, 0)),
            pl.BlockSpec((3, heads, count), lambda h: (0, 0, 0)),
        ],
        out_shape=[
            jax.ShapeDtypeStruct((2, heads, HD, count // 2), F32),
            jax.ShapeDtypeStruct((3, heads, count), F32),
        ],
        compiler_params=params(),
        cost_estimate=cost(16 * heads * count * tokens * HD, 9e6),
        name="attend",
    )(q, k, v, u)


def backward_kernel(
    chunk, q_ref, k_ref, v_ref, u_ref, stat_ref, dq_ref, dkv_ref, done_ref
):
    head = pl.program_id(0)
    count = q_ref.shape[2]
    half = count // 2
    keys_t = k_ref[0]
    keys = keys_t.astype(F32).T.astype(BF16)
    vals = v_ref[0].astype(F32).T.astype(BF16)
    key_grad = jnp.zeros(keys.shape, F32)
    value_grad = jnp.zeros(vals.shape, F32)
    total = stat_ref[1, pl.ds(head, 1), :]
    lse = stat_ref[0, pl.ds(head, 1), :] + jnp.log(total)
    delta = stat_ref[2, pl.ds(head, 1), :] / total
    for start in range(0, count, chunk):
        cols = slice(start, start + chunk)
        q = q_ref[0, :, cols]
        u = u_ref[0, :, cols]
        probs = jnp.exp(dot(keys, q) - lse[:, cols])
        grad = (probs * (dot(vals, u) - delta[:, cols])).astype(BF16)
        value_grad += dot(probs.astype(BF16), u.astype(F32).T.astype(BF16))
        key_grad += dot(grad, q.astype(F32).T.astype(BF16))
        side, inner = divmod(start, half)
        dq_ref[side, 0, :, inner : inner + chunk] = dot(keys_t, grad)
    dkv_ref[0, 0] = key_grad.T.astype(BF16)
    dkv_ref[1, 0] = value_grad.T.astype(BF16)
    done_ref[...] = jnp.zeros_like(done_ref)


def backward(q, k, v, u, stats):
    heads, _, count = q.shape
    tokens = k.shape[2]
    per_head = lambda n: pl.BlockSpec((1, HD, n), lambda h: (h, 0, 0))
    return pl.pallas_call(
        functools.partial(backward_kernel, min(256, count // 2)),
        grid=(heads,),
        in_specs=[
            per_head(count), per_head(tokens), per_head(tokens), per_head(count),
            pl.BlockSpec((3, heads, count), lambda h: (0, 0, 0)),
        ],
        out_specs=[
            pl.BlockSpec((2, 1, HD, count // 2), lambda h: (0, h, 0, 0)),
            pl.BlockSpec((2, 1, HD, tokens), lambda h: (0, h, 0, 0)),
            pl.BlockSpec((8, 128), lambda h: (0, 0)),
        ],
        out_shape=[
            jax.ShapeDtypeStruct((2, heads, HD, count // 2), F32),
            jax.ShapeDtypeStruct((2, heads, HD, tokens), BF16),
            jax.ShapeDtypeStruct((8, 128), F32),
        ],
        compiler_params=params(),
        cost_estimate=cost(40 * heads * count * tokens * HD, 9e6),
        name="attend_back",
    )(q, k, v, u, stats)


def sum_kernel(pieces_ref, after_ref, out_ref):
    out_ref[...] = jnp.sum(pieces_ref[...], 0)


def sum_pieces(pieces, after):
    return pl.pallas_call(
        sum_kernel,
        out_shape=jax.ShapeDtypeStruct(pieces.shape[1:], F32),
        compiler_params=params(),
        cost_estimate=cost(pieces.size, 4 * pieces.size),
        name="sum_pieces",
    )(pieces, after)


def out_kernel(att_ref, rows_ref, own_ref, other_ref, grad_ref, keep_ref, send_ref):
    att = att_ref[0].reshape(own_ref.shape[1], att_ref.shape[3]).astype(BF16)
    term = dot(rows_ref[...], att, NT)

    @pl.when(pl.program_id(0) == 0)
    def _():
        grad_ref[...] = term

    @pl.when(pl.program_id(0) > 0)
    def _():
        grad_ref[...] += term

    send_ref[...] = dot(other_ref[...], att)
    keep_ref[...] = dot(own_ref[...], att)


def out_step(att, rows, own, other):
    _, heads, _, half = att.shape
    width, inner = own.shape
    share = rows.shape[0]
    whole = lambda a: pl.BlockSpec(a.shape, lambda i: (0, 0))
    return pl.pallas_call(
        out_kernel,
        grid=(2,),
        in_specs=[
            pl.BlockSpec((1, heads, HD, half), lambda i: (i, 0, 0, 0)),
            pl.BlockSpec((share, half), lambda i: (0, i)),
            whole(own),
            whole(other),
        ],
        out_specs=[
            pl.BlockSpec((share, inner), lambda i: (0, 0)),
            pl.BlockSpec((width, half), lambda i: (0, i)),
            pl.BlockSpec((width, half), lambda i: (0, i)),
        ],
        out_shape=[
            jax.ShapeDtypeStruct((share, inner), F32),
            jax.ShapeDtypeStruct((width, 2 * half), F32),
            jax.ShapeDtypeStruct((width, 2 * half), F32),
        ],
        compiler_params=params(),
        cost_estimate=cost(8 * half * inner * width, 12e6),
        name="project_out",
    )(att, rows, own, other)


def query_kernel(pieces_ref, norm_ref, out_ref):
    places, share, _ = out_ref.shape
    heads = places // 2
    total = jnp.sum(pieces_ref[...], 0)
    depth, half = total.shape
    rows = half // heads
    proj = (total * HD ** (-0.5)).astype(BF16)
    term = dot(norm_ref[...], proj, NT)
    for place in range(places):
        strip = place % heads * rows
        out_ref[place, :, :depth] = term[place * share : (place + 1) * share, :]
        out_ref[place, :depth, 128 : 128 + rows] = total[:, strip : strip + rows]


def query_step(pieces, norm, places):
    _, depth, half = pieces.shape
    width = norm.shape[0]
    return pl.pallas_call(
        query_kernel,
        out_shape=jax.ShapeDtypeStruct((places, width // places, 256), F32),
        compiler_params=params(),
        cost_estimate=cost(2 * half * width * depth, 6e6),
        name="query_grad",
    )(pieces, norm)


def latent_kernel(pieces_ref, qw_ref, latents_ref, cot_ref, out_ref):
    heads, depth, rows = pieces_ref.shape
    proj = pieces_ref[...].reshape(heads * depth, rows) * HD ** (-0.5)
    up = dot(proj.T.astype(BF16), qw_ref[...])
    hat, inv = layer_norm(latents_ref[...].astype(F32))
    term = norm_backward(hat, inv, up) + cot_ref[...].astype(F32) / 2
    size = out_ref.shape[2]
    for block in range(out_ref.shape[0]):
        out_ref[block] = term[:, block * size : (block + 1) * size]


def latent_step(pieces, qw, latents, cot, blocks):
    rows, width = latents.shape
    return pl.pallas_call(
        latent_kernel,
        out_shape=jax.ShapeDtypeStruct((blocks, rows, width // blocks), F32),
        compiler_params=params(),
        cost_estimate=cost(2 * rows * qw.size, 4e6),
        name="latent_grad",
    )(pieces, qw, latents, cot)


def shift(value, axis, by, side=None, minor=True):
    size = lax.axis_size(axis)
    if side is None:
        pairs = [(i, (i + by) % size) for i in range(size)]
    elif minor:
        pairs = [(i, i // side * side + (i % side + by) % side) for i in range(size)]
    else:
        pairs = [(i, (i + by * side) % size) for i in range(size)]
    return lax.ppermute(value, axis, pairs)


def pick(blocks, index):
    return lax.dynamic_index_in_dim(blocks, index, 0, False)


def scatter_sum(blocks, axis, place):
    size = blocks.shape[0]
    total = pick(blocks, place)
    for by in range(1, size):
        total = total + shift(pick(blocks, (place + by) % size), axis, by)
    return total


def relay_sum(blocks, place, cut, send):
    far = pick(blocks, (place + 2) % 4)
    front = send(far[:cut], 1)
    back = send(far[cut:], -1)
    ahead = pick(blocks, (place + 1) % 4)
    behind = pick(blocks, (place + 3) % 4)
    ahead = jnp.concatenate([ahead[:cut] + front, ahead[cut:]], 0)
    behind = jnp.concatenate([behind[:cut], behind[cut:] + back], 0)
    return pick(blocks, place) + send(ahead, 1) + send(behind, -1)


def merge_stats(stats, side, minor):
    parts = [stats] + [shift(stats, "seq", by, side, minor) for by in range(1, side)]
    top = functools.reduce(jnp.maximum, [p[0] for p in parts])
    factors = [jnp.exp(p[0] - top) for p in parts]
    total = sum(p[1] * f for p, f in zip(parts, factors))
    delta = sum(p[2] * f for p, f in zip(parts, factors))
    return jnp.stack([top, total, delta])


def local(media_tokens, latents, query_weight, key_weight, value_weight, out_weight, cotangent):
    inner = query_weight.shape[1]
    width = query_weight.shape[0]
    heads = inner // HD
    count = latents.shape[0]
    half = count // 2
    seq, tp, dp = (lax.axis_index(a) for a in ("seq", "tp", "dp"))
    seqs, tps, dps = (lax.axis_size(a) for a in ("seq", "tp", "dp"))
    side = 4
    share = width // seqs
    part = share // dps
    padded = -(-part // 8) * 8
    rows = count // seqs
    upstream = cotangent[0]
    query_turned = query_weight.T

    media_norm, latent_norm, k, v, q, u = project(
        media_tokens[0], latents, upstream, query_turned, key_weight.T, value_weight.T, out_weight
    )
    weighted, stats = forward(q, k, v, u)

    whole = merge_stats(merge_stats(stats, side, True), side, False)
    factor = (jnp.exp(stats[0] - whole[0]) / whole[1]).reshape(heads, 2, 1, half).transpose(1, 0, 2, 3)

    scaled = (weighted * factor).reshape(seqs, HD, half)
    attended_pieces = lax.all_to_all(scaled, "seq", 0, 0, tiled=True)
    dq, dkv, done = backward(q, k, v, u, whole)
    seq, tp, done = lax.optimization_barrier((seq, tp, done))

    query_pieces = lax.all_to_all(dq.reshape(seqs, HD, half), "seq", 0, 0, tiled=True)

    blocks = media_norm.reshape(seqs, dps, part, -1).transpose(1, 0, 2, 3)
    blocks = jnp.pad(blocks, ((0, 0), (0, 0), (0, padded - part), (0, 0)))
    term = dot(blocks.reshape(dps * seqs * padded, -1), dkv.reshape(2 * inner, -1), NT)
    term = term.reshape(dps, seqs * padded, 2 * inner)
    term = relay_sum(term, dp, seqs * padded // 2, lambda value, by: shift(value, "dp", by))
    term = lax.all_to_all(term.reshape(seqs, padded, 2 * inner), "seq", 0, 0, tiled=True)
    term = jnp.sum(term, 0)[:part]
    grad_key, grad_value = term[:, :inner], term[:, inner:]

    attended = lax.all_gather(sum_pieces(attended_pieces, done), "seq")
    cot_cols = lax.dynamic_slice_in_dim(upstream, seq * share, share, 1).T
    own = lax.dynamic_slice_in_dim(out_weight, tp * inner, inner, 1).T
    other = lax.dynamic_slice_in_dim(out_weight, (1 - tp) * inner, inner, 1).T
    latent_cols = lax.dynamic_slice_in_dim(latents, tp * inner, inner, 1).T
    out_rows, keep, away = out_step(attended.reshape(2, heads, HD, half), cot_cols, own, other)
    arrived = lax.ppermute(away, "tp", [(0, 1), (1, 0)])
    resampled = (latent_cols.astype(F32) + (keep + arrived)).astype(BF16).T[None]
    grad_out = scatter_sum(out_rows.reshape(dps, part, inner), "dp", dp).T

    side_of = seq // heads
    norm_half = lax.dynamic_slice_in_dim(latent_norm, side_of * half, half, 1)
    sent = query_step(query_pieces, norm_half, seqs)
    sent = lax.all_to_all(sent, "seq", 0, 0, tiled=True)
    strips = lax.dynamic_slice(sent, (side_of * heads, 0, 128), (heads, HD, rows))
    latent_rows = lax.dynamic_slice_in_dim(latents, seq * rows, rows, 0)
    cot_rows = lax.dynamic_slice_in_dim(upstream, seq * rows, rows, 0)
    term = latent_step(strips, query_turned, latent_rows, cot_rows, tps * dps)
    blocks = (sent[:heads, :, :HD] + sent[heads:, :, :HD]).transpose(1, 0, 2)
    grad_query = scatter_sum(blocks.reshape(dps, part, inner), "dp", dp)
    grad_latents = jnp.sum(lax.all_to_all(term, ("tp", "dp"), 0, 0, tiled=True), 0)
    return (resampled, grad_latents, grad_query, grad_key, grad_value, grad_out)


def solution(mesh):
    placed = (
        P("dp", "seq", None),
        P(),
        P(None, "tp"),
        P(None, "tp"),
        P(None, "tp"),
        P("tp", None),
        P("dp", None, None),
    )
    return jax.shard_map(
        local,
        mesh=mesh,
        in_specs=placed,
        out_specs=(
            P("dp", None, "tp"),
            P("seq", ("tp", "dp")),
            P(("seq", "dp"), "tp"),
            P(("seq", "dp"), "tp"),
            P(("seq", "dp"), "tp"),
            P("tp", ("seq", "dp")),
        ),
        check_vma=False,
    )
```
